32 devices in a mesh: section: 2 (over y), group: 8 (over z, core), shard: 2 (over x).
Axes of the slice: x: 2, y: 2, z: 4, core: 2. Of those that a mesh axis runs over, the one named last changes fastest.
Arguments:
- block_input: bfloat16 [8192, 768], P(('group', 'shard')), may hold values from -6 to 6
- cotangent: bfloat16 [8192, 768], P(('group', 'shard')), may hold values from -8 to 8
- lengths: int32 [16], replicated, may hold values from 64 to 512, as said below
- assignment: int32 [16, 1], replicated, may hold values from 0 to 3
- qkv_weight: bfloat16 [2, 768, 2304], P('section'), may hold values from -0.3125 to 0.3125
- out_weight: bfloat16 [2, 768, 768], P('section'), may hold values from -1.25 to 1.25
- in_weight: bfloat16 [2, 768, 3072], P('section'), may hold values from -0.21875 to 0.21875
- back_weight: bfloat16 [2, 3072, 768], P('section'), may hold values from -0.15625 to 0.15625
- attn_bias: bfloat16 [2, 3, 768], P('section'), may hold values from -1.25 to 1.25
- norm_gain: bfloat16 [2, 2, 768], P('section'), may hold values from 0.5 to 1.5
- norm_shift: bfloat16 [2, 2, 768], P('section'), may hold values from -1.25 to 1.25
- in_bias: bfloat16 [2, 3072], P('section'), may hold values from -1.75 to 1.75
- back_bias: bfloat16 [2, 768], P('section'), may hold values from -1.25 to 1.25
Outputs:
- layer_outputs: bfloat16 [2, 8192, 768], P('section', ('group', 'shard'))
- layer_input_grads: bfloat16 [2, 8192, 768], P('section', ('group', 'shard'))
- grad_qkv_weight: float32 [2, 768, 2304], P('section', None, 'shard')
- grad_out_weight: float32 [2, 768, 768], P('section', None, 'shard')
- grad_in_weight: float32 [2, 768, 3072], P('section', None, 'shard')
- grad_back_weight: float32 [2, 3072, 768], P('section', None, 'shard')
- grad_attn_bias: float32 [2, 3, 768], P('section', None, 'shard')
- grad_norm_gain: float32 [2, 2, 768], P('section', None, 'shard')
- grad_norm_shift: float32 [2, 2, 768], P('section', None, 'shard')
- grad_in_bias: float32 [2, 3072], P('section', 'shard')
- grad_back_bias: float32 [2, 768], P('section', 'shard')
The draws below stay inside these ranges and needn't reach their ends.
Inputs may be any that keep to these rules, and one draw needn't show every extreme that they name: `lengths`: every read has 64 to 512 live tokens, and all reads of some data device have 512. `assignment`: every one of the 4 micro-batches holds at least one read.
All inputs are finite; a program needn't handle non-finite values.
Results may differ from the reference program's by a relative error of at most 0.03.
Values may be sent and summed in bfloat16 or wider, within the bound.
No kernel may reach another device: no remote copies, remote signals or barrier semaphores. Data moves between devices by JAX's collectives and lax.ppermute only.
A program may use at most 256 MiB of HBM per device.

```python
import math
import jax
import jax.numpy as jnp
from jax import lax

D = 768
HEADS = 12
HEAD_DIM = 64
FF = 3072
SEQ = 512
MIN_LEN = 64
MICRO = 4
READS_DEV = 1
READS = 16
TOKENS = 8192


def draw_lengths(key, part):
    key = jax.random.fold_in(key, 11)
    first_key, second_key = jax.random.split(key)
    drawn = jax.random.randint(first_key, (READS,), MIN_LEN, SEQ + 1)
    full_device = jax.random.randint(second_key, (), 0, READS // READS_DEV)
    read_owner = jnp.arange(READS) // READS_DEV
    return jnp.where(read_owner == full_device, SEQ, drawn).astype(jnp.int32)


def strengthened(entries, key, source, target, parts, factor):
    def block_of(axis_at):
        return (jnp.arange(entries.shape[axis_at]) // (entries.shape[axis_at] // parts)).reshape((-1,) + (1,) * (entries.ndim - 1 - axis_at))

    near = jax.random.permutation(key, parts)[block_of(target)]
    second = (block_of(target) + parts // 2) % parts
    return jnp.where((block_of(source) == near) | (block_of(source) == second), factor * entries, entries)


def shard_levels(key, shape, cuts, smallest, high):
    loudness = 1.0
    for axis_at, shards_of in cuts:
        heights = jax.random.uniform(jax.random.fold_in(jax.random.fold_in(key, 6), axis_at), (shards_of,), jnp.float32, smallest / len(cuts), high / len(cuts))
        loudness = loudness * jnp.repeat(jnp.exp(heights), shape[axis_at] // shards_of).reshape((-1,) + (1,) * (len(shape) - 1 - axis_at))
    return loudness


def picks_of(rng, rows, amount, top, lift):
    ranking = jax.random.permutation(jax.random.fold_in(rng, 1), amount)
    pull = ranking
    for power in range(3):
        pull = pull * pull // amount
    pull = pull * lift // amount
    chance = jax.random.randint(jax.random.fold_in(rng, 2), (rows, amount), 0, 4096) + pull
    sure = jax.random.permutation(jax.random.fold_in(rng, 3), rows)[jnp.arange(amount) % rows]
    chance = jnp.where(jnp.arange(rows)[:, None] == sure[None, :], 1 << 14, chance)
    priority = chance * amount + jnp.arange(amount)
    return lax.top_k(priority.astype(jnp.int32), top)[1].astype(jnp.int32)


def noise(rng, dims, scale, limit, cuts=(), kind=jnp.bfloat16):
    values = scale * jax.random.normal(rng, dims, jnp.float32)
    if cuts:
        values = values * shard_levels(rng, dims, cuts, -0.22, 0.18)
    return jnp.clip(values, -limit, limit).astype(kind)


def heavy_noise(key, shape, deviation, limit, cuts, heavy, held_as=jnp.bfloat16):
    values = deviation * jax.random.normal(key, shape, jnp.float32)
    if cuts:
        values = values * shard_levels(key, shape, cuts, -0.22, 0.18)
    return jnp.clip(strengthened(values, jax.random.fold_in(key, 3), *heavy), -limit, limit).astype(held_as)


def setup_inputs(seed: int = 0) -> dict:
    key_of = jax.random.split(jax.random.key(seed), 14)
    block_input = noise(key_of[0], (TOKENS, D), 1.0, 6.0, ((0, 16),))
    cotangent = heavy_noise(key_of[1], (TOKENS, D), 1.0, 8.0, ((0, 16),), (0, 1, 16, 2.0))
    lengths = draw_lengths(jax.random.fold_in(key_of[13], 71), 0)
    assignment = picks_of(key_of[3], READS, MICRO, 1, 4096)
    qkv_weight = noise(key_of[4], (2, D, 3 * D), (D // 2) ** -0.5, 0.3125, ((0, 2),))
    out_weight = noise(key_of[5], (2, D, D), (D // 32) ** -0.5, 1.25, ((0, 2),))
    in_weight = noise(key_of[6], (2, D, FF), D ** -0.5, 0.21875, ((0, 2),))
    back_weight = noise(key_of[7], (2, FF, D), (FF // 2) ** -0.5, 0.15625, ((0, 2),))
    attn_bias = noise(key_of[8], (2, 3, D), 0.2, 1.25, ((0, 2),))
    norm_gain = jnp.clip(1.0 + 0.1 * jax.random.normal(key_of[9], (2, 2, D), jnp.float32), 0.5, 1.5).astype(jnp.bfloat16)
    norm_shift = noise(key_of[10], (2, 2, D), 0.2, 1.25, ((0, 2),))
    in_bias = noise(key_of[11], (2, FF), 0.3, 1.75, ((0, 2),))
    back_bias = noise(key_of[12], (2, D), 0.2, 1.25, ((0, 2),))
    return dict(block_input=block_input, cotangent=cotangent, lengths=lengths, assignment=assignment, qkv_weight=qkv_weight, out_weight=out_weight, in_weight=in_weight, back_weight=back_weight, attn_bias=attn_bias, norm_gain=norm_gain, norm_shift=norm_shift, in_bias=in_bias, back_bias=back_bias)


@jax.custom_vjp
def low(v):
    return lax.optimization_barrier(v.astype(jnp.bfloat16)).astype(jnp.float32)

@jax.custom_vjp
def low_back(v):
    return v

def low_keep(v):
    return (low(v), None)

def low_pass(kept, grad):
    return (grad,)

def back_keep(v):
    return (v, None)

def back_low(kept, grad):
    return (low(grad),)
low.defvjp(low_keep, low_pass)
low_back.defvjp(back_keep, back_low)
norm_eps = 1e-12
masked_score = -1e+30

def matmul(left, right):
    return jnp.dot(left, right, precision=lax.Precision.HIGHEST, preferred_element_type=jnp.float32)

def layer_norm(summed, norm_gain, norm_shift):
    row_mean = lax.optimization_barrier(jnp.mean(summed, axis=-1, keepdims=True))
    centred = summed - row_mean
    variance = lax.optimization_barrier(jnp.mean(centred * centred, axis=-1, keepdims=True))
    return centred * lax.rsqrt(variance + norm_eps) * norm_gain + norm_shift

def exact_gelu(values):
    return jax.nn.gelu(values, approximate=False)

def read_weights(lengths, assignment):
    member = assignment[:, 0:1] == jnp.arange(MICRO, dtype=jnp.int32)[None, :]
    counts = lax.optimization_barrier(jnp.sum(jnp.where(member, lengths[:, None], 0), axis=0))
    token_total = jnp.sum(lengths).astype(jnp.float32)
    scales = token_total / (MICRO * counts.astype(jnp.float32))
    return lax.optimization_barrier(jnp.sum(jnp.where(member, scales[None, :], 0.0), axis=1))

def attend(qkv_read, length):
    queries = qkv_read[:, :D].reshape(SEQ, HEADS, HEAD_DIM)
    key_rows = qkv_read[:, D:2 * D].reshape(SEQ, HEADS, HEAD_DIM)
    values = qkv_read[:, 2 * D:].reshape(SEQ, HEADS, HEAD_DIM)
    scores = jnp.einsum('qhd,khd->hqk', queries, key_rows, precision=lax.Precision.HIGHEST) / math.sqrt(HEAD_DIM)
    scores = low_back(scores)
    key_live = jnp.arange(SEQ) < length
    scores = jnp.where(key_live[None, None, :], scores, masked_score)
    top_score = lax.optimization_barrier(jnp.max(scores, axis=-1, keepdims=True))
    exp_scores = jnp.exp(scores - top_score)
    attention = low(exp_scores / lax.optimization_barrier(jnp.sum(exp_scores, axis=-1, keepdims=True)))
    context = jnp.einsum('hqk,khd->qhd', attention, values, precision=lax.Precision.HIGHEST)
    return context.reshape(SEQ, D)
attend_saved = jax.checkpoint(attend)

def encoder_layer(inputs, block_lengths, qkv_weight, out_weight, in_weight, back_weight, attn_bias, norm_gain, norm_shift, in_bias, back_bias):
    qkv_bias = jnp.concatenate([attn_bias[0], jnp.zeros_like(attn_bias[0]), attn_bias[1]])
    qkv_rows = low_back(low(matmul(inputs, qkv_weight) + qkv_bias))
    context = lax.map(lambda paired: attend_saved(paired[0], paired[1]), (qkv_rows.reshape(-1, SEQ, 3 * D), block_lengths))
    context = low_back(low(context.reshape(-1, D)))
    branch = low_back(matmul(context, out_weight) + attn_bias[2])
    normed_one = layer_norm(inputs + branch, norm_gain[0], norm_shift[0])
    hidden = low_back(matmul(low(normed_one), in_weight) + in_bias)
    active = low(exact_gelu(hidden))
    ffn_out = low_back(matmul(active, back_weight) + back_bias)
    return layer_norm(normed_one + ffn_out, norm_gain[1], norm_shift[1])

def reference(block_input, cotangent, lengths, assignment, qkv_weight, out_weight, in_weight, back_weight, attn_bias, norm_gain, norm_shift, in_bias, back_bias):
    group_reads = math.gcd(READS, 8)
    block_count = READS // group_reads
    scales = read_weights(lengths, assignment)
    stacked = tuple((array_item.astype(jnp.float32) for array_item in (qkv_weight, out_weight, in_weight, back_weight, attn_bias, norm_gain, norm_shift, in_bias, back_bias)))
    first_params = tuple((array_item[0] for array_item in stacked))
    second_params = tuple((array_item[1] for array_item in stacked))
    input_blocks = block_input.astype(jnp.float32).reshape(block_count, group_reads * SEQ, D)
    cot_blocks = (cotangent.astype(jnp.float32).reshape(READS, SEQ, D) * scales[:, None, None]).reshape(block_count, group_reads * SEQ, D)
    length_blocks = lengths.reshape(block_count, group_reads)

    def step_block(carried, pieces):
        inputs, cot_rows, block_lengths = pieces
        probe_rows = jnp.zeros_like(inputs)

        def forward(inputs, probe_rows, first_params, second_params):
            row_mask = (jnp.arange(SEQ)[None, :] < block_lengths[:, None]).reshape(-1, 1).astype(jnp.float32)
            first_out = encoder_layer(inputs, block_lengths, *first_params) * row_mask
            sent_rows = low_back(low(first_out)) + probe_rows
            second_out = encoder_layer(sent_rows, block_lengths, *second_params) * row_mask
            return (jnp.sum(cot_rows * second_out), (low(first_out), second_out))
        loss_value, back_fn, extras = jax.vjp(forward, inputs, probe_rows, first_params, second_params, has_aux=True)
        d_inputs, d_probe, d_first, d_second = back_fn(jnp.ones_like(loss_value))
        carried = jax.tree.map(jnp.add, carried, (d_first, d_second))
        return (carried, (extras[0].astype(jnp.bfloat16), extras[1].astype(jnp.bfloat16), d_inputs.astype(jnp.bfloat16), d_probe.astype(jnp.bfloat16)))
    start = jax.tree.map(jnp.zeros_like, (first_params, second_params))
    carried, outputs = lax.scan(step_block, start, (input_blocks, cot_blocks, length_blocks))
    grads = jax.tree.map(lambda one_grad, two_grad: jnp.stack([one_grad, two_grad]), carried[0], carried[1])
    layer_outputs = jnp.stack([outputs[0].reshape(TOKENS, D), outputs[1].reshape(TOKENS, D)])
    layer_input_grads = jnp.stack([outputs[2].reshape(TOKENS, D), outputs[3].reshape(TOKENS, D)])
    return (layer_outputs, layer_input_grads, grads[0], grads[1], grads[2], grads[3], grads[4], grads[5], grads[6], grads[7], grads[8])
```

```python
from functools import partial

import jax
import jax.numpy as jnp
from jax import lax
from jax.experimental import pallas as pl
from jax.experimental.pallas import tpu as pltpu
from jax.sharding import Mesh, PartitionSpec as P

D = 768
HEADS = 12
HEAD_DIM = 64
FF = 3072
SEQ = 512
MICRO = 4

norm_eps = 1e-12
masked_score = -1e30
f32 = jnp.float32
bf16 = jnp.bfloat16
MIB = 1024 * 1024
FT = 512
RB = 256
UNIT = D // 2

SECTION, Z, CORE, SHARD = "section", "z", "core", "shard"
DATA = (Z, CORE, SHARD)
SWAP = [(0, 1), (1, 0)]

HBM = pl.BlockSpec(memory_space=pltpu.HBM)
ANY = pl.BlockSpec(memory_space=pl.ANY)
VM = pl.BlockSpec(memory_space=pltpu.VMEM)
SM = pl.BlockSpec(memory_space=pltpu.SMEM)


def sds(shape, dtype):
    return jax.ShapeDtypeStruct(shape, dtype)


def dot(a, b, ca=1, cb=0):
    return lax.dot_general(a, b, (((ca,), (cb,)), ((), ())), preferred_element_type=f32)


def params(mib):
    return pltpu.CompilerParams(vmem_limit_bytes=mib * MIB)


def cost(flops, bytes_accessed):
    return pl.CostEstimate(flops=flops, bytes_accessed=bytes_accessed, transcendentals=0)


def dma_sems(count):
    return pltpu.SemaphoreType.DMA((count,))


class Box:
    def __init__(self, names=(), refs=()):
        for n, r in zip(names, refs):
            setattr(self, n, r)

    def __getattr__(self, name):
        return None


def names_of(*tables):
    return [n for t in tables for n in t]


def shapes_of(*tables):
    return [sds(*e) for t in tables for e in t.values()]


def scratch_of(*tables, without=()):
    merged = {n: e for t in reversed(tables) for n, e in t.items() if n not in without}
    return list(merged), [pltpu.VMEM(*e) for e in merged.values()]


class Copies:
    def __init__(self, sems):
        self.sems, self.pending = sems, []

    def put(self, src, dst):
        if dst is not None:
            c = pltpu.make_async_copy(src, dst, self.sems.at[len(self.pending)])
            c.start()
            self.pending.append(c)

    def wait(self):
        for c in self.pending:
            c.wait()


def load(sems, **pairs):
    loads = Box()
    for i, (name, (src, dst)) in enumerate(pairs.items()):
        setattr(loads, name, pltpu.make_async_copy(src, dst, sems.at[i]))
        getattr(loads, name).start()
    return loads


def arrived(*copies):
    for c in copies:
        if c is not None:
            c.wait()


def live_rows(length, rows, cols, start=0):
    return lax.broadcasted_iota(jnp.int32, (rows, cols), 0) + start < length


def column_sum(v):
    return jnp.sum(v, axis=0, keepdims=True)


def gelu_and_slope(h):
    phi = 0.5 + 0.5 * lax.erf(h * 0.7071067811865476)
    return h * phi, phi + h * (jnp.exp(-0.5 * (h * h)) * 0.3989422804014327)


def qkv_step(x, wqkv, ab, qkv_t, loads):
    for j, ready in enumerate((loads.wq, loads.wk, loads.wv)):
        arrived(ready)
        part = dot(x[...], wqkv[:, j * D : (j + 1) * D])
        if j == 0:
            part = part + ab[0:1, :].astype(f32)
        elif j == 2:
            part = part + ab[1:2, :].astype(f32)
        low = part.astype(bf16)
        if j == 0:
            low = low * jnp.bfloat16(0.125)
        qkv_t[j * D : (j + 1) * D, :] = low.T


def head_rows(part, h):
    return slice(part * D + h * HEAD_DIM, part * D + (h + 1) * HEAD_DIM)


def attention_step(length, qkv_t, scores, expo, inv, ctx_t):
    dead_keys = lax.broadcasted_iota(jnp.int32, (16, SEQ), 1) >= length
    first_row = lax.broadcasted_iota(jnp.int32, (16, SEQ), 0) == 0
    mask_row = jnp.where(dead_keys & first_row, masked_score, 0.0).astype(bf16)
    one_row = jnp.where(first_row, 1.0, 0.0).astype(bf16)

    def score(h):
        k = jnp.concatenate([qkv_t[head_rows(1, h), :], mask_row], axis=0)
        q = jnp.concatenate([qkv_t[head_rows(0, h), :], one_row], axis=0)
        scores[h % 2] = dot(k, q, 0, 0)

    def context(h):
        c = dot(qkv_t[head_rows(2, h), :], expo[h]) * inv[h : h + 1, :]
        ctx_t[head_rows(0, h), :] = c.astype(bf16)

    score(0)
    for h in range(HEADS):
        if h + 1 < HEADS:
            score(h + 1)
        if h > 0:
            context(h - 1)
        for b in range(SEQ // RB):
            cols = slice(b * RB, (b + 1) * RB)
            s = scores[h % 2, :, cols]
            e = jnp.exp(s - jnp.max(s, axis=0, keepdims=True))
            inv[h : h + 1, cols] = 1.0 / column_sum(e)
            expo[h, :, cols] = e.astype(bf16)
    context(HEADS - 1)


def norm_rows(summed):
    centred = summed - jnp.mean(summed, axis=-1, keepdims=True)
    rstd = lax.rsqrt(jnp.mean(centred * centred, axis=-1, keepdims=True) + norm_eps)
    return centred * rstd, rstd


def first_norm_step(x, ctx_t, wout, ab, ng, ns, xh1, r1, first, nlow):
    for b in range(SEQ // RB):
        rows = slice(b * RB, (b + 1) * RB)
        summed = x[rows, :].astype(f32) + dot(ctx_t[:, rows].T, wout[...]) + ab[2:3, :].astype(f32)
        xh, rstd = norm_rows(summed)
        xh1[rows, :] = xh
        r1[rows, :] = jnp.broadcast_to(rstd, (RB, 128))
        one = xh * ng[0:1, :].astype(f32) + ns[0:1, :].astype(f32)
        first[rows, :] = one
        nlow[rows, :] = one.astype(bf16)


def feed_forward_step(nlow, win, wback, ib, hidden, act, slope, acc):
    count = FF // FT

    def into(f):
        cols = slice(f * FT, (f + 1) * FT)
        hidden[f % 2] = dot(nlow[...], win[:, cols]) + ib[:, cols].astype(f32)

    into(0)
    for f in range(count):
        cols = slice(f * FT, (f + 1) * FT)
        if f + 1 < count:
            into(f + 1)
        a, g = gelu_and_slope(hidden[f % 2])
        act[:, cols] = a.astype(bf16)
        if slope is not None:
            slope[:, cols] = g.astype(bf16)
    acc[...] = dot(act[...], wback[...])


def second_norm_step(length, first, acc, bb, ng, ns, xh2, r2, out):
    for b in range(SEQ // RB):
        rows = slice(b * RB, (b + 1) * RB)
        xh, rstd = norm_rows(first[rows, :] + acc[rows, :] + bb[...].astype(f32))
        xh2[rows, :] = xh
        r2[rows, :] = jnp.broadcast_to(rstd, (RB, 128))
        y = xh * ng[1:2, :].astype(f32) + ns[1:2, :].astype(f32)
        out[rows, :] = jnp.where(live_rows(length, RB, D, b * RB), y, 0.0).astype(bf16)


def norm_back(d, xh, rstd, gain):
    gd = d * gain.astype(f32)
    m1 = jnp.mean(gd, axis=-1, keepdims=True)
    m2 = jnp.mean(gd * xh, axis=-1, keepdims=True)
    return (gd - m1 - xh * m2) * rstd


def second_norm_back_step(length, d_rows, scale, xh2, r2, ng, acc, dmixed, small):
    small[...] = jnp.zeros((16, D), f32)
    for b in range(SEQ // RB):
        rows = slice(b * RB, (b + 1) * RB)
        dy = jnp.where(live_rows(length, RB, D, b * RB), d_rows[rows, :].astype(f32) * scale, 0.0)
        xh = xh2[rows, :]
        small[1:2, :] += column_sum(dy * xh)
        small[3:4, :] += column_sum(dy)
        d2 = norm_back(dy, xh, r2[rows, 0:1], ng[1:2, :])
        acc[rows, :] = d2
        low = d2.astype(bf16)
        dmixed[rows, :] = low
        small[4:5, :] += column_sum(low.astype(f32))


def feed_back_step(dmixed, wback, win, slope, dh, acc, small, arrive, leave):
    for f in range(FF // FT):
        cols = slice(f * FT, (f + 1) * FT)
        arrive(f)
        low = (dot(dmixed[...], wback[cols, :], 1, 1) * slope[:, cols].astype(f32)).astype(bf16)
        dh[:, cols] = low
        sums = column_sum(low.astype(f32))
        for piece in range(0, FT, RB):
            at = f * FT + piece
            small[8 + at // D : 9 + at // D, at % D : at % D + RB] = sums[:, piece : piece + RB]
    leave()
    acc[...] += dot(dh[...], win[...], 1, 1)


def first_norm_back_step(acc, xh1, r1, ng, dsum, dbranch, small):
    for b in range(SEQ // RB):
        rows = slice(b * RB, (b + 1) * RB)
        df = acc[rows, :]
        xh = xh1[rows, :]
        small[0:1, :] += column_sum(df * xh)
        small[2:3, :] += column_sum(df)
        d1 = norm_back(df, xh, r1[rows, 0:1], ng[0:1, :])
        dsum[rows, :] = d1
        low = d1.astype(bf16)
        dbranch[rows, :] = low
        small[5:6, :] += column_sum(low.astype(f32))


def context_back_step(wout, dbranch, dctx_t):
    dctx_t[...] = dot(wout[...], dbranch[...], 1, 1).astype(bf16)


def attention_back_step(heads, qkv_t, expo, inv, ctx_t, dctx_t, dprob, dqkv_t, arrive=lambda h: None):
    kept = {}

    def into(h):
        d_o = dctx_t[head_rows(0, h), :].astype(f32) * inv[h : h + 1, :]
        delta = column_sum(d_o * ctx_t[head_rows(0, h), :].astype(f32))
        low = d_o.astype(bf16)
        dprob[h % 2] = dot(qkv_t[head_rows(2, h), :], low, 0, 0)
        kept[h] = (low, delta)

    def out_of(h):
        low, delta = kept.pop(h)
        arrive(h)
        p = expo[h]
        ds = (p.astype(f32) * (dprob[h % 2] - delta)).astype(bf16)
        d_q = (dot(qkv_t[head_rows(1, h), :], ds) * 0.125).astype(bf16)
        d_k = dot(qkv_t[head_rows(0, h), :], ds, 1, 1).astype(bf16)
        dqkv_t[head_rows(0, h), :] = d_q
        dqkv_t[head_rows(1, h), :] = d_k
        dqkv_t[head_rows(2, h), :] = dot(low, p, 1, 1).astype(bf16)

    heads = list(heads)
    into(heads[0])
    for i, h in enumerate(heads):
        if i + 1 < len(heads):
            into(heads[i + 1])
        out_of(h)


def qkv_back_step(dqkv_t, dqkv, small):
    for j in range(3):
        low = dqkv_t[j * D : (j + 1) * D, :].T
        dqkv[:, j * D : (j + 1) * D] = low
        if j != 1:
            at = 6 + j // 2
            small[at : at + 1, :] = column_sum(low.astype(f32))


def input_back_step(dqkv, wqkv, dsum, din):
    for b in range(SEQ // RB):
        rows = slice(b * RB, (b + 1) * RB)
        din[rows, :] = (dot(dqkv[rows, :], wqkv[...], 1, 1) + dsum[rows, :]).astype(bf16)


ROWS16 = ((SEQ, D), bf16)
ROWS32 = ((SEQ, D), f32)
COLS16 = ((D, SEQ), bf16)
STD = ((SEQ, 128), f32)
WIDE16 = ((SEQ, FF), bf16)
QKV_T = ((3 * D, SEQ), bf16)
EXPO = ((HEADS, SEQ, SEQ), bf16)
INV = ((16, SEQ), f32)
SCORES = ((2, SEQ, SEQ), f32)
SMALL = ((16, D), f32)
HALF = ((SEQ, D // 2), bf16)
HALF_T = ((D // 2, SEQ), bf16)

OUT = dict(out=ROWS16)
SHARED = dict(
    x_own=HALF, x_send=HALF, ctx_own=HALF_T, ctx_send=HALF_T, nlow=ROWS16, act_own=((SEQ, FF // 2), bf16),
    act_send=((SEQ, FF // 2), bf16),
)
STORED = dict(
    qkv_t=QKV_T, expo=EXPO, inv=INV, ctx_t=COLS16, xh1=ROWS32, r1=STD, slope=WIDE16, xh2=ROWS32, r2=STD
)
NORM_OUTS = dict(dmixed=ROWS16)
BLOCK2 = ((2, SEQ, UNIT), bf16)
FFN_OUTS = dict(
    dh0=HALF, dh1=HALF, dh2=HALF, dh3=HALF, ds0=HALF, ds1=HALF, ds2=HALF, ds3=HALF, dbranch=ROWS16
)
ATT_OUTS = dict(
    dqkv0=BLOCK2, dqkv1=BLOCK2, dqkv2=BLOCK2, small=SMALL
)
DIN = dict(din=ROWS16)
NORM_MORE = dict(acc=ROWS32, small=SMALL)
FFN_MORE = dict(dctx_t=COLS16, dsum=ROWS32, small=SMALL)

WEIGHTS = dict(wqkv=((D, 3 * D), bf16), wout=((D, D), bf16), win=((D, FF), bf16), wback=((FF, D), bf16))
FORWARD = dict(
    x=ROWS16, qkv_t=QKV_T, scores=SCORES, expo=EXPO, inv=INV, ctx_t=COLS16, nlow=ROWS16, xh1=ROWS32, r1=STD,
    first=ROWS32, act=WIDE16, slope=WIDE16, xh2=ROWS32, r2=STD, out=ROWS16, acc=ROWS32,
)
BACK_FFN = dict(
    acc=ROWS32, dmixed=ROWS16, dh=WIDE16, dsum=ROWS32, dbranch=ROWS16, dctx_t=COLS16, small=SMALL
)
BACK_ATT = dict(dqkv_t=QKV_T, dqkv=((SEQ, 3 * D), bf16), din=ROWS16)


def halves(core, width):
    return (
        pl.ds(pl.multiple_of(core * width, 128), width),
        pl.ds(pl.multiple_of((1 - core) * width, 128), width),
    )


def weight_loads(v, wqkv, wout, win, wback):
    parts = [pl.ds(j * D, D) for j in range(3)]
    wq, wk, wv = [(wqkv.at[:, p], v.wqkv.at[:, p]) for p in parts]
    return dict(wq=wq, wk=wk, wv=wv, wout=(wout, v.wout), win=(win, v.win), wback=(wback, v.wback))


def forward_steps(v, w, o, length, core, copies, loads):
    own_d, other_d = halves(core, D // 2)
    own_f, other_f = halves(core, FF // 2)
    arrived(loads.x)
    copies.put(v.x.at[:, own_d], o.x_own)
    copies.put(v.x.at[:, other_d], o.x_send)
    qkv_step(v.x, v.wqkv, w.ab, v.qkv_t, loads)
    copies.put(v.qkv_t, o.qkv_t)
    attention_step(length, v.qkv_t, v.scores, v.expo, v.inv, v.ctx_t)
    copies.put(v.ctx_t.at[own_d, :], o.ctx_own)
    copies.put(v.ctx_t.at[other_d, :], o.ctx_send)
    copies.put(v.expo, o.expo)
    copies.put(v.inv, o.inv)
    copies.put(v.ctx_t, o.ctx_t)
    arrived(loads.wout)
    first_norm_step(v.x, v.ctx_t, v.wout, w.ab, w.ng, w.ns, v.xh1, v.r1, v.first, v.nlow)
    copies.put(v.nlow, o.nlow)
    copies.put(v.xh1, o.xh1)
    copies.put(v.r1, o.r1)
    arrived(loads.win, loads.wback)
    feed_forward_step(v.nlow, v.win, v.wback, w.ib, v.scores, v.act, v.slope, v.acc)
    copies.put(v.act.at[:, own_f], o.act_own)
    copies.put(v.act.at[:, other_f], o.act_send)
    copies.put(v.slope, o.slope)
    second_norm_step(length, v.first, v.acc, w.bb, w.ng, w.ns, v.xh2, v.r2, v.out)
    copies.put(v.out, o.out)
    copies.put(v.xh2, o.xh2)
    copies.put(v.r2, o.r2)


def leave_hidden(dh, o, core, copies):
    for refs, c in (((o.ds0, o.ds1, o.ds2, o.ds3), 1 - core), ((o.dh0, o.dh1, o.dh2, o.dh3), core)):
        for i, ref in enumerate(refs):
            half, block = i // 2, i % 2
            at = pl.multiple_of(half * (FF // 2) + c * (FF // 4) + block * UNIT, 128)
            copies.put(dh.at[:, pl.ds(at, UNIT)], ref)


def ffn_back_steps(v, w, o, core, copies):
    def leave():
        leave_hidden(v.dh, o, core, copies)

    feed_back_step(v.dmixed, v.wback, v.win, v.slope, v.dh, v.acc, v.small, lambda f: None, leave)
    first_norm_back_step(v.acc, v.xh1, v.r1, w.ng, v.dsum, v.dbranch, v.small)
    copies.put(v.dbranch, o.dbranch)
    context_back_step(v.wout, v.dbranch, v.dctx_t)


def leave_dqkv(v, o, copies):
    for u, ref in enumerate((o.dqkv0, o.dqkv1, o.dqkv2)):
        for half in range(2):
            copies.put(v.dqkv.at[:, pl.ds((3 * half + u) * UNIT, UNIT)], ref.at[half])
    copies.put(v.small, o.small)


def attention_back_end(v, o, copies):
    qkv_back_step(v.dqkv_t, v.dqkv, v.small)
    leave_dqkv(v, o, copies)
    input_back_step(v.dqkv, v.wqkv, v.dsum, v.din)
    copies.put(v.din, o.din)


SMALL_WEIGHTS = dict(ab=0, ng=0, ns=0, ib=0, bb=0)


def here(lengths):
    z, core, shard = lax.axis_index(Z), lax.axis_index(CORE), lax.axis_index(SHARD)
    read = (z * 2 + core) * lax.axis_size(SHARD) + shard
    return jnp.where(lax.axis_index(SECTION) == 0, 1, 0), lengths[read], core


def first_kernel(names, out_names, lengths, x, wqkv, wout, win, wback, ab, ng, ns, ib, bb, *rest):
    n = len(out_names)
    o = Box(out_names, rest[:n])
    v = Box(names, rest[n:-2])
    w = Box(SMALL_WEIGHTS, (ab, ng, ns, ib, bb))
    live, length, core = here(lengths)

    @pl.when(live == 1)
    def _():
        loads = load(rest[-2], x=(x, v.x), **weight_loads(v, wqkv, wout, win, wback))
        copies = Copies(rest[-1])
        forward_steps(v, w, o, length, core, copies, loads)
        copies.wait()


def first_forward(lengths, x, weights, tables, name):
    without = () if STORED in tables else ("slope",)
    names, scratch = scratch_of(WEIGHTS, FORWARD, without=without)
    outs = shapes_of(*tables)
    return pl.pallas_call(
        partial(first_kernel, names, names_of(*tables)),
        out_shape=outs,
        in_specs=[SM, ANY] + [HBM] * 4 + [VM] * 5,
        out_specs=[HBM] * len(outs),
        scratch_shapes=scratch + [dma_sems(7), dma_sems(len(outs))],
        compiler_params=params(54),
        cost_estimate=cost(8 * 10**9, 36 * 10**6),
        name=name,
    )(lengths, x, *weights)


SECOND_OUTS = (OUT, SHARED, NORM_OUTS, FFN_OUTS, ATT_OUTS, DIN)


def second_kernel(names, scal, scale, x, cot, wqkv, wout, win, wback, ab, ng, ns, ib, bb, *rest):
    rest = rest[1 + len(SHARED) :]
    out_names = names_of(*SECOND_OUTS)
    n = len(out_names)
    o = Box(out_names, rest[:n])
    v = Box(names, rest[n:-2])
    w = Box(SMALL_WEIGHTS, (ab, ng, ns, ib, bb))

    @pl.when(scal[0] == 1)
    def _():
        length, core = scal[1], scal[2]
        loads = load(rest[-2], x=(x, v.x), **weight_loads(v, wqkv, wout, win, wback), cot=(cot, v.cot))
        copies = Copies(rest[-1])
        v.dsum, v.dh, v.dqkv_t = v.first, v.slope, v.qkv_t
        forward_steps(v, w, o, length, core, copies, loads)
        arrived(loads.cot)
        second_norm_back_step(length, v.cot, scale[0], v.xh2, v.r2, w.ng, v.acc, v.dmixed, v.small)
        copies.put(v.dmixed, o.dmixed)
        ffn_back_steps(v, w, o, core, copies)
        attention_back_step(range(HEADS), v.qkv_t, v.expo, v.inv, v.ctx_t, v.dctx_t, v.scores, v.dqkv_t)
        attention_back_end(v, o, copies)
        copies.wait()


def second_layer(scal, scale, x, cot, weights, shared):
    names, scratch = scratch_of(
        WEIGHTS, FORWARD, BACK_FFN, BACK_ATT, dict(cot=ROWS16), without=("dsum", "dh", "dqkv_t")
    )
    outs = shapes_of(*SECOND_OUTS)
    n_in = 13
    flat = pl.pallas_call(
        partial(second_kernel, names),
        out_shape=outs,
        in_specs=[SM, SM, ANY, ANY] + [HBM] * 4 + [VM] * 5 + [HBM] * len(shared),
        out_specs=[HBM] * len(outs),
        input_output_aliases={n_in + i: i for i in range(len(shared))},
        scratch_shapes=scratch + [dma_sems(8), dma_sems(len(outs) + 5)],
        compiler_params=params(57),
        cost_estimate=cost(20 * 10**9, 36 * 10**6),
        name="second_layer",
    )(scal, scale, x, cot, *weights, *shared)
    return Box(names_of(*SECOND_OUTS), flat)


def pick(source, table):
    return [getattr(source, n) for n in table]


def in_hbm(arrays):
    return [pltpu.with_memory_space_constraint(a, pltpu.HBM) for a in arrays]


def take_late(pairs, sems):
    copies = Copies(sems)
    for src, dst in pairs:
        copies.put(src, dst)
    copies.wait()


def norm_back_kernel(scal, d_rows, xh2, r2, ng, late, dmixed, acc, small, sems):
    @pl.when(scal[0] == 1)
    def _():
        second_norm_back_step(scal[1], d_rows, 1.0, xh2, r2, ng, acc, dmixed, small)

    @pl.when(scal[0] == 0)
    def _():
        take_late([(late, dmixed)], sems)


def first_norm_back(scal, d_rows, given, late):
    outs = shapes_of(NORM_OUTS, NORM_MORE)
    flat = pl.pallas_call(
        norm_back_kernel,
        out_shape=outs,
        in_specs=[SM, VM, VM, VM, VM, HBM],
        out_specs=[VM] * len(outs),
        scratch_shapes=[dma_sems(1)],
        compiler_params=params(8),
        cost_estimate=cost(10**7, 6 * 10**6),
        name="first_norm_back",
    )(scal, d_rows, given.xh2, given.r2, given.ng, *in_hbm([late.dmixed]))
    return flat[0], Box(NORM_MORE, flat[1:])


FFN_LOADS = dict(dmixed=0, win=0, acc=0, small=0, r1=0, wout=0, ng=0)
FFN_LATER = dict(wback=0, slope=0, xh1=0)


def ffn_back_kernel(scal, *rest):
    given = Box(names_of(FFN_LOADS, FFN_LATER), rest)
    rest = rest[len(FFN_LOADS) + len(FFN_LATER) :]
    late = rest[: len(FFN_OUTS)]
    rest = rest[len(FFN_OUTS) :]
    o = Box(names_of(FFN_OUTS, FFN_MORE), rest)
    dh, acc, wback, xh1, tile_sems, sems = rest[-6:]

    @pl.when(scal[0] == 1)
    def _():
        core = scal[2]
        tiles = []
        for f in range(FF // FT):
            part = pl.ds(f * FT, FT)
            for src, dst in (
                (given.wback.at[part, :], wback.at[part, :]), (given.slope.at[:, part], dh.at[:, part])
            ):
                tiles.append(pltpu.make_async_copy(src, dst, tile_sems.at[len(tiles)]))
                tiles[-1].start()
        last = load(tile_sems.at[pl.ds(len(tiles), 1)], xh1=(given.xh1, xh1))
        copies = Copies(sems)
        acc[...] = given.acc[...]
        o.small[...] = given.small[...]

        def leave():
            leave_hidden(dh, o, core, copies)

        def arrive(f):
            arrived(tiles[2 * f], tiles[2 * f + 1])

        feed_back_step(given.dmixed, wback, given.win, dh, dh, acc, o.small, arrive, leave)
        arrived(last.xh1)
        first_norm_back_step(acc, xh1, given.r1, given.ng, o.dsum, o.dbranch, o.small)
        context_back_step(given.wout, o.dbranch, o.dctx_t)
        copies.wait()

    @pl.when(scal[0] == 0)
    def _():
        take_late(zip(late, pick(o, FFN_OUTS)), sems)


def first_ffn_back(scal, given, late):
    outs = shapes_of(FFN_OUTS, FFN_MORE)
    flat = pl.pallas_call(
        ffn_back_kernel,
        out_shape=outs,
        in_specs=[SM] + [VM] * len(FFN_LOADS) + [HBM] * (len(FFN_LATER) + len(FFN_OUTS)),
        out_specs=[VM] * len(outs),
        scratch_shapes=[
            pltpu.VMEM(*WIDE16), pltpu.VMEM(*ROWS32), pltpu.VMEM(*WEIGHTS["wback"]), pltpu.VMEM(*ROWS32),
            dma_sems(2 * FF // FT + 1), dma_sems(len(FFN_OUTS)),
        ],
        compiler_params=params(22),
        cost_estimate=cost(6 * 10**9, 25 * 10**6),
        name="first_ffn_back",
    )(scal, *pick(given, FFN_LOADS), *in_hbm(pick(given, FFN_LATER)), *in_hbm(pick(late, FFN_OUTS)))
    n = len(FFN_OUTS)
    return Box(FFN_OUTS, flat), Box(FFN_MORE, flat[n:])


ATT_FIRST = dict(qkv_t=0, expo=0, inv=0, ctx_t=0, dctx_t=0)
ATT_LATER = dict(small=0)


def att_early_kernel(heads, scal, qkv_t, expo, inv, ctx_t, dctx_t, out, dqkv_t, dprob):
    @pl.when(scal[0] == 1)
    def _():
        attention_back_step(heads, qkv_t, expo, inv, ctx_t, dctx_t, dprob, dqkv_t)
        size = len(heads) * HEAD_DIM
        for p in range(3):
            low = p * D + heads[0] * HEAD_DIM
            out[p * size : (p + 1) * size, :] = dqkv_t[low : low + size, :]


def first_att_back_early(scal, heads, given):
    return pl.pallas_call(
        partial(att_early_kernel, heads),
        out_shape=sds((3 * len(heads) * HEAD_DIM, SEQ), bf16),
        in_specs=[SM] + [VM] * len(ATT_FIRST),
        out_specs=VM,
        scratch_shapes=[pltpu.VMEM(*QKV_T), pltpu.VMEM(*SCORES)],
        compiler_params=params(10),
        cost_estimate=cost(0, 0),
        name="first_att_back_early",
    )(scal, *pick(given, ATT_FIRST))


def att_end_kernel(names, heads, scal, *rest):
    given = Box(names_of(ATT_FIRST, ATT_LATER), rest)
    rest = rest[len(ATT_FIRST) + len(ATT_LATER) :]
    early, late, rest = rest[0], rest[1 : 1 + len(ATT_OUTS)], rest[1 + len(ATT_OUTS) :]
    o = Box(ATT_OUTS, rest)
    v = Box(names, rest[len(ATT_OUTS) : -1])

    @pl.when(scal[0] == 1)
    def _():
        g = given
        attention_back_step(heads, g.qkv_t, g.expo, g.inv, g.ctx_t, g.dctx_t, v.scores, v.dqkv_t)
        size = heads[0] * HEAD_DIM
        for p in range(3):
            v.dqkv_t[p * D : p * D + size, :] = early[p * size : (p + 1) * size, :]
        v.small[...] = g.small[...]
        copies = Copies(rest[-1])
        qkv_back_step(v.dqkv_t, v.dqkv, v.small)
        leave_dqkv(v, o, copies)
        copies.wait()

    @pl.when(scal[0] == 0)
    def _():
        stages = [v.dqkv.at[:, pl.ds(i * UNIT, UNIT)] for i in range(6)] + [v.small]
        before = [late[u].at[half] for u in range(3) for half in range(2)] + list(late[3:])
        there = [r.at[half] for r in (o.dqkv0, o.dqkv1, o.dqkv2) for half in range(2)] + [o.small]
        take_late(zip(before, stages), rest[-1])
        take_late(zip(stages, there), rest[-1])


def first_att_back(scal, heads, given, early, late):
    names, scratch = scratch_of(BACK_ATT, dict(scores=SCORES, small=SMALL), without=("din",))
    outs = [pltpu.HBM(*e) for e in ATT_OUTS.values()]
    flat = pl.pallas_call(
        partial(att_end_kernel, names, heads),
        out_shape=outs,
        in_specs=[SM] + [VM] * (len(ATT_FIRST) + len(ATT_LATER) + 1) + [HBM] * len(ATT_OUTS),
        out_specs=[HBM] * len(outs),
        scratch_shapes=scratch + [dma_sems(len(outs) + 3)],
        compiler_params=params(18),
        cost_estimate=cost(0, 0),
        name="first_att_back",
    )(scal, *pick(given, ATT_FIRST), *pick(given, ATT_LATER), early, *in_hbm(pick(late, ATT_OUTS)))
    return Box(ATT_OUTS, flat)


def input_back_kernel(scal, d0, d1, d2, wqkv, dsum, late, din, dqkv, w, ds, stage, sems):
    @pl.when(scal[0] == 1)
    def _():
        copies = Copies(sems)
        for u, ref in enumerate((d0, d1, d2)):
            for half in range(2):
                copies.put(ref.at[half], dqkv.at[:, pl.ds((3 * half + u) * UNIT, UNIT)])
        copies.put(wqkv, w)
        copies.put(dsum, ds)
        copies.wait()
        input_back_step(dqkv, w, ds, stage)

    @pl.when(scal[0] == 0)
    def _():
        take_late([(late, stage)], sems)

    take_late([(stage, din)], sems)


def first_input_back(scal, dqkv, wqkv, dsum, late):
    return pl.pallas_call(
        input_back_kernel,
        out_shape=pltpu.HBM(*ROWS16),
        in_specs=[SM] + [HBM] * 6,
        out_specs=HBM,
        scratch_shapes=[
            pltpu.VMEM((SEQ, 3 * D), bf16), pltpu.VMEM(*WEIGHTS["wqkv"]), pltpu.VMEM(*ROWS32), pltpu.VMEM(*ROWS16),
            dma_sems(8),
        ],
        compiler_params=params(16),
        cost_estimate=cost(0, 0),
        name="first_input_back",
    )(scal, *in_hbm(dqkv), *in_hbm([wqkv, dsum, late]))


def half_of_small(small, h):
    rows = [small[0:8, h * UNIT : (h + 1) * UNIT]]
    for j in range(4):
        at = h * (FF // 2) + j * UNIT
        rows.append(small[8 + at // D : 9 + at // D, at % D : at % D + UNIT])
    rows.append(jnp.zeros((4, UNIT), f32))
    return jnp.concatenate(rows, axis=0)


def grad_kernel(pieces, n_in, scal, *refs):
    ins, outs = refs[:n_in], refs[n_in:]
    keep_at = scal[3]
    for out, half in zip(outs, (1 - keep_at, keep_at)):
        at = 0
        for a1, a2, a_dim, a_start, a_size, b1, b2, b_start in pieces:
            block = slice(a_start, a_start + a_size)

            def left(i):
                return ins[i][:, block] if a_dim == 0 else ins[i][block, :]

            def right(i):
                if isinstance(i, tuple):
                    return jnp.where(half == 0, ins[i[0]][...], ins[i[1]][...])
                width = ins[i].shape[1] // 2
                return ins[i][:, pl.ds(pl.multiple_of(half * width + b_start, 128), UNIT)]

            total = dot(left(a1), right(b1), a_dim, 0) + dot(left(a2), right(b2), a_dim, 0)
            out[at : at + a_size, :] = total.astype(bf16)
            at += a_size


def grad_chunk(scal, operands, pieces, name):
    rows = sum(p[4] for p in pieces)
    return pl.pallas_call(
        partial(grad_kernel, pieces, len(operands)),
        out_shape=[sds((rows, UNIT), bf16)] * 2,
        in_specs=[SM] + [VM] * len(operands),
        out_specs=[VM] * 2,
        compiler_params=params(10),
        cost_estimate=cost(2 * 2 * SEQ * rows * UNIT * 2, 6 * 10**6),
        name=name,
    )(scal, *operands)


def last_grads_kernel(scal, *refs):
    blocks, others = refs[7:13], refs[:7]
    sides = refs[13:17]
    stages, b, sems = refs[17:24], refs[24], refs[25]
    x1, x2, c1, c2, db1, db2, small = stages
    first, units, rest = Copies(sems.at[pl.ds(0, 2)]), Copies(sems.at[pl.ds(2, 6)]), Copies(sems.at[pl.ds(8, 5)])
    for i in range(2):
        first.put(others[i], stages[i])
    for u in range(3):
        for i in range(2):
            units.put(blocks[3 * i + u], b.at[u, i])
    for i in range(2, 7):
        rest.put(others[i], stages[i])
    keep_at = scal[3]
    sides = tuple(zip((1 - keep_at, keep_at), sides[0:2], sides[2:4]))
    first.wait()
    for u in range(3):
        arrived(*units.pending[2 * u : 2 * u + 2])
        for half, *outs in sides:
            total = dot(x1[...], b[u, 0, half], 0, 0) + dot(x2[...], b[u, 1, half], 0, 0)
            outs[u // 2][u % 2 * UNIT : (u % 2 + 1) * UNIT, :] = total.astype(bf16)
    rest.wait()
    for half, _, out in sides:
        cols = pl.ds(pl.multiple_of(half * UNIT, 128), UNIT)
        out[UNIT : 2 * UNIT, :] = (dot(c1[...], db1[:, cols]) + dot(c2[...], db2[:, cols])).astype(bf16)
        out[2 * UNIT : 2 * UNIT + 16, :] = jnp.where(half == 0, half_of_small(small[...], 0), half_of_small(small[...], 1)).astype(bf16)


def last_grads(scal, others, blocks):
    stages = (HALF, HALF, HALF_T, HALF_T, ROWS16, ROWS16, SMALL)
    return pl.pallas_call(
        last_grads_kernel,
        out_shape=[sds((2 * UNIT, UNIT), bf16)] * 2 + [sds((2 * UNIT + 16, UNIT), bf16)] * 2,
        in_specs=[SM] + [ANY] * 13,
        out_specs=[VM] * 4,
        scratch_shapes=[pltpu.VMEM(*e) for e in stages]
        + [pltpu.VMEM((3, 2, 2, SEQ, UNIT), bf16), dma_sems(13)],
        compiler_params=params(18),
        cost_estimate=cost(0, 0),
        name="last_grads",
    )(scal, *others, *blocks)


def place_kernel(moves, n_prev, n_out, scal, own, other, *rest):
    outs = rest[n_prev : n_prev + n_out]
    stage, sem = rest[-2:]
    core = scal[2]
    copies = Copies(sem)
    for i, (ref, c) in enumerate(((own, core), (other, 1 - core))):
        stage[i] = ref[...].astype(f32)
        for out, src, size, rows, row_step, col, col_step in moves:
            row = pl.multiple_of(rows + c * row_step, 8)
            column = pl.multiple_of(col + c * col_step, 128)
            copies.put(stage.at[i, pl.ds(src, size), :], outs[out].at[pl.ds(row, size), pl.ds(column, UNIT)])
    if n_out < len(rest) - 2 - n_prev:
        bias, gain, shift, hidden, last = rest[n_prev + n_out : -2]
        at = own.shape[0] - 16
        small = own[at : at + 16, :].astype(f32) + other[at : at + 16, :].astype(f32)
        gain[...] = small[0:2, :]
        shift[...] = small[2:4, :]
        last[...] = small[4:5, :]
        bias[0:1, :] = small[6:7, :]
        bias[1:2, :] = small[7:8, :]
        bias[2:3, :] = small[5:6, :]
        for j in range(4):
            hidden[:, j * UNIT : (j + 1) * UNIT] = small[8 + j : 9 + j, :]
    copies.wait()


SMALL_OUTS = ((3, UNIT), (2, UNIT), (2, UNIT), (1, FF // 2), (1, UNIT))


def place(scal, own, other, moves, shapes, previous, with_small=False):
    kept = [i for i, p in enumerate(previous) if p is not None]
    small = [sds(s, f32) for s in SMALL_OUTS] if with_small else []
    return pl.pallas_call(
        partial(place_kernel, moves, len(kept), len(shapes)),
        out_shape=[sds(s, f32) for s in shapes] + small,
        in_specs=[SM, VM, VM] + [HBM] * len(kept),
        out_specs=[HBM] * len(shapes) + [VM] * len(small),
        input_output_aliases={3 + j: i for j, i in enumerate(kept)},
        scratch_shapes=[pltpu.VMEM((2,) + own.shape, f32), dma_sems(2 * len(moves))],
        compiler_params=params(8),
        cost_estimate=cost(0, own.size * 12),
        name="place",
    )(scal, own, other, *[previous[i] for i in kept])


def add_kernel(start, a, b, out):
    rows = slice(start, start + out.shape[0])
    out[...] = (a[rows, :].astype(f32) + b[rows, :].astype(f32)).astype(bf16)


def added(a, b, start=0, size=None):
    rows = slice(start, start + (a.shape[0] if size is None else size))
    return (a[rows].astype(f32) + b[rows].astype(f32)).astype(bf16)


def take_kernel(takes, a, b, out):
    @pl.when(takes[0] == 1)
    def _():
        out[...] = a[...]

    @pl.when(takes[0] == 0)
    def _():
        out[...] = b[...]


def taken(takes, a, b):
    return jnp.where(takes[0] == 1, a, b)


def read_weights(lengths, assignment):
    member = assignment == jnp.arange(MICRO, dtype=jnp.int32)[None, :]
    counts = jnp.sum(jnp.where(member, lengths[:, None], 0), axis=0)
    token_total = jnp.sum(lengths).astype(f32)
    scales = token_total / (MICRO * counts.astype(f32))
    return jnp.sum(jnp.where(member, scales[None, :], 0.0), axis=1)


class Order:
    def __init__(self):
        self.last = None

    def after(self, value):
        if self.last is not None:
            value, self.last = lax.optimization_barrier((value, self.last))
        return value

    def done(self, value):
        self.last = value
        return value


class Sums:
    def __init__(self, scal, order, z_index, z_count, shapes):
        self.scal, self.order, self.z_index, self.z_count, self.shapes = scal, order, z_index, z_count, shapes
        self.value, self.moving, self.keep, self.results, self.small = {}, {}, {}, {}, None
        half = z_count // 2
        self.stages = [[self.shard_done, partial(self.inward, hop=0)]]
        for hop in range(half - 1):
            self.stages.append([self.add, self.middle if hop + 2 == half else partial(self.inward, hop=hop + 1)])
        self.stages.append([self.add, partial(self.outward, hop=half - 2)])
        for hop in range(half - 2, -1, -1):
            after = partial(self.outward, hop=hop - 1) if hop > 0 else self.core
            self.stages.append([partial(self.take, hop=hop), after])
        self.stages.append([self.place])

    def start(self, pair, sizes):
        moving, at = lax.ppermute(pair[0], SHARD, SWAP), 0
        for size in sizes:
            i = len(self.keep)
            self.keep[i], self.moving[i] = pair[1], (moving, at, size)
            at += size

    def tick(self, t):
        for stage, steps in enumerate(self.stages):
            for i in range(len(PLACES)):
                if t == i + stage - (stage == 0 and i > 3):
                    for step in steps:
                        step(i)

    def shard_done(self, i):
        moving, at, size = self.moving[i]
        self.value[i] = self.order.done(added(self.order.after(moving), self.keep[i], at, size))

    def inward(self, i, hop):
        last = self.z_count - 1
        self.moving[i] = lax.ppermute(self.value[i], Z, [(hop, hop + 1), (last - hop, last - 1 - hop)])

    def add(self, i):
        self.value[i] = self.order.done(added(self.value[i], self.order.after(self.moving[i])))

    def middle(self, i):
        half = self.z_count // 2
        self.moving[i] = lax.ppermute(self.value[i], Z, [(half - 1, half), (half, half - 1)])

    def outward(self, i, hop):
        last = self.z_count - 1
        self.moving[i] = lax.ppermute(self.value[i], Z, [(hop + 1, hop), (last - 1 - hop, last - hop)])

    def take(self, i, hop):
        takes = ((self.z_index == hop) | (self.z_index == self.z_count - 1 - hop)).astype(jnp.int32)[None]
        self.value[i] = self.order.done(taken(takes, self.order.after(self.moving[i]), self.value[i]))

    def core(self, i):
        self.moving[i] = lax.ppermute(self.value[i], CORE, SWAP)

    def place(self, i):
        targets, moves, with_small = PLACES[i]
        flat = place(
            self.scal, self.value[i], self.order.after(self.moving[i]), moves, [self.shapes[t] for t in targets],
            [self.results.get(t) for t in targets], with_small,
        )
        self.order.done(flat[0])
        for t, r in zip(targets, flat):
            self.results[t] = r
        if with_small:
            self.small = flat[len(targets) :]


G_BACK, G_IN, G_QKV, G_OUT = range(4)
PLACES = (
    ((G_BACK,), ((0, 0, D, 0, FF // 2, 0, 0),), False),
    ((G_BACK,), ((0, 0, D, D, FF // 2, 0, 0),), False),
    ((G_IN,), ((0, 0, D, 0, 0, 0, FF // 4),), False),
    ((G_IN,), ((0, 0, D, 0, 0, UNIT, FF // 4),), False),
    ((G_QKV,), ((0, 0, UNIT, 0, UNIT, 0, 0), (0, UNIT, UNIT, 0, UNIT, UNIT, 0)), False),
    ((G_QKV, G_OUT), ((0, 0, UNIT, 0, UNIT, 2 * UNIT, 0), (1, UNIT, UNIT, 0, UNIT, 0, 0)), True),
)


def sums_by_collectives(pairs, small, shard, shard_count):
    side = [[p[1] for p in pairs], [p[0] for p in pairs]]
    back = jnp.concatenate([jnp.concatenate(s[0:2], axis=0) for s in side], axis=1)
    inner = jnp.stack([jnp.concatenate([s[2][:D], s[2][D:]], axis=1) for s in side], axis=1)
    qkv = jnp.concatenate([part for s in side for part in (s[3][:UNIT], s[3][UNIT:], s[4][:UNIT])], axis=1)
    out = jnp.concatenate([s[4][UNIT : 2 * UNIT] for s in side], axis=1)

    def mine(whole):
        width = whole.shape[1] // shard_count
        return lax.dynamic_slice_in_dim(whole, shard * width, width, 1)

    def by_rows(quarter):
        return mine(lax.all_gather(lax.psum(quarter.astype(f32), (Z, SHARD)), CORE, axis=0, tiled=True))

    inner = lax.all_gather(lax.psum(inner.astype(f32), (Z, SHARD)), CORE, axis=2).reshape(D, FF)
    total = lax.psum(small, DATA)
    part = mine(total)
    hidden = mine(total[8:12].reshape(1, FF))
    results = {G_BACK: by_rows(back), G_IN: mine(inner), G_QKV: by_rows(qkv), G_OUT: by_rows(out)}
    return results, (jnp.stack([part[6], part[7], part[5]]), part[0:2], part[2:4], hidden, part[4:5])


def body(
    block_input, cotangent, lengths, assignment, qkv_weight, out_weight, in_weight, back_weight, attn_bias, norm_gain,
    norm_shift, in_bias, back_bias,
):
    section = lax.axis_index(SECTION)
    z_index, core, shard = lax.axis_index(Z), lax.axis_index(CORE), lax.axis_index(SHARD)
    z_count, shard_count = lax.axis_size(Z), lax.axis_size(SHARD)
    weights = (
        qkv_weight[0], out_weight[0], in_weight[0], back_weight[0], attn_bias[0], norm_gain[0], norm_shift[0], in_bias,
        back_bias,
    )
    keep_at = shard if shard_count == 2 else 0
    (out,) = first_forward(lengths, block_input, weights, (OUT,), "first_forward")
    received = lax.ppermute(out, SECTION, [(0, 1)])
    lengths, assignment, _ = lax.optimization_barrier((lengths, assignment, out))
    data_index = (z_index * 2 + core) * shard_count + shard
    length = lax.dynamic_index_in_dim(lengths, data_index, 0, keepdims=False)
    own_scale = lax.dynamic_slice_in_dim(read_weights(lengths, assignment), data_index, 1)

    def scalars(live):
        return jnp.stack([live.astype(jnp.int32), length, core, jnp.asarray(keep_at, jnp.int32)])

    def core_swap(array):
        return lax.ppermute(array, CORE, SWAP)

    at_first, at_second = scalars(section == 0), scalars(section == 1)
    kept = first_forward(lengths, block_input, weights, (SHARED, STORED), "first_forward_kept")
    given = Box(names_of(SHARED, STORED), kept)
    late = second_layer(at_second, own_scale, *in_hbm([received]), cotangent, weights, [out, *kept[: len(SHARED)]])
    returned = lax.ppermute(late.din, SECTION, [(1, 0)])
    from_peer = [core_swap(a) for a in (late.act_send, late.nlow, late.x_send, late.ctx_send)]
    returned, from_peer = lax.optimization_barrier((returned, from_peer))
    act_peer, nlow_peer, x_peer, ctx_peer = from_peer

    order = Order()
    shapes = {
        G_QKV: (D, 3 * D // shard_count), G_OUT: (D, D // shard_count), G_IN: (D, FF // shard_count),
        G_BACK: (FF, D // shard_count),
    }
    sums = Sums(at_first, order, z_index, z_count, shapes)
    pairs = []

    def start(pair, sizes):
        pairs.append(pair)
        if shard_count == 2:
            sums.start(pair, sizes)

    def grad(operands, pieces, name):
        pair = grad_chunk(order.after(at_first), operands, pieces, name)
        order.done(pair[0])
        start(pair, (D,) * len(pieces))

    def tick(*args):
        if shard_count == 2:
            sums.tick(*args)

    given.ng, given.wqkv, given.wout, given.win, given.wback = norm_gain[0], *weights[:4]
    given.dmixed, more = first_norm_back(at_first, returned, given, late)
    given.acc, given.small = more.acc, more.small
    dmixed_peer = core_swap(given.dmixed)
    for k in range(2):
        grad((late.act_own, act_peer, given.dmixed, dmixed_peer), ((0, 1, 0, k * D, D, 2, 3, 0),), "grad_back")
    ffn, more = first_ffn_back(order.after(at_first), given, late)
    order.done(ffn.dbranch)
    given.dctx_t, given.dsum, given.small = more.dctx_t, more.dsum, more.small
    own = (ffn.dh0, ffn.dh1, ffn.dh2, ffn.dh3)
    peer = [core_swap(a) for a in (ffn.ds0, ffn.ds1, ffn.ds2, ffn.ds3)]
    tick(0)
    operands = (late.nlow, nlow_peer, *own, *peer)
    grad(operands, ((0, 1, 0, 0, D, (2, 4), (6, 8), 0), (0, 1, 0, 0, D, (3, 5), (7, 9), 0)), "grad_in")
    dbranch_peer = core_swap(ffn.dbranch)
    cut = HEADS - 2
    early = order.done(first_att_back_early(order.after(at_first), range(cut), given))
    tick(1)
    go, dbranch_peer = order.after((at_first, dbranch_peer))
    att = first_att_back(go, range(cut, HEADS), given, early, late)
    order.done(att.small)
    own = (att.dqkv0, att.dqkv1, att.dqkv2)
    peer = [core_swap(a) for a in own]

    x_own, ctx_own = in_hbm([late.x_own, late.ctx_own])
    others = (x_own, x_peer, ctx_own, ctx_peer, ffn.dbranch, dbranch_peer, att.small)
    last = last_grads(order.after(at_first), others, (*in_hbm(own), *peer))
    order.done(last[0])
    start(last[0:2], (D,))
    start(last[2:4], (D + 16,))
    if shard_count == 2:
        for t in range(2, len(PLACES) + len(sums.stages) - 1):
            tick(t)
            if t == 7:
                din = order.done(first_input_back(order.after(at_first), own, weights[0], given.dsum, late.din))
        results, small = sums.results, sums.small
    else:
        din = first_input_back(at_first, own, weights[0], given.dsum, late.din)
        results, small = sums_by_collectives(pairs, att.small, shard, shard_count)
    return (
        late.out[None], din[None], results[G_QKV][None], results[G_OUT][None], results[G_IN][None],
        results[G_BACK][None], small[0][None], small[1][None], small[2][None], small[3], small[4],
    )


def solution(mesh):
    sections, groups, shards = mesh.devices.shape
    mesh = Mesh(mesh.devices.reshape(sections, groups // 2, 2, shards), (SECTION, Z, CORE, SHARD))
    rows, layers, pairs = P(DATA, None), P(SECTION, None, None), P(SECTION, None)
    both, columns = P(SECTION, DATA, None), P(SECTION, None, SHARD)
    in_specs = (rows, rows, P(), P()) + (layers,) * 7 + (pairs,) * 2
    out_specs = (both, both) + (columns,) * 7 + (P(SECTION, SHARD),) * 2
    return jax.shard_map(body, mesh=mesh, in_specs=in_specs, out_specs=out_specs, check_vma=False)
```

```python
from functools import partial

import jax
import jax.numpy as jnp
from jax import lax
from jax.experimental import pallas as pl
from jax.experimental.pallas import tpu as pltpu
from jax.sharding import Mesh, PartitionSpec as P

D = 768
HEADS = 12
HEAD_DIM = 64
FF = 3072
SEQ = 512
MICRO = 4

norm_eps = 1e-12
masked_score = -1e30
f32 = jnp.float32
bf16 = jnp.bfloat16
MIB = 1024 * 1024
FT = 512
RB = 256
UNIT = D // 2

SECTION, Z, CORE, SHARD = "section", "z", "core", "shard"
DATA = (Z, CORE, SHARD)
SWAP = [(0, 1), (1, 0)]

HBM = pl.BlockSpec(memory_space=pltpu.HBM)
ANY = pl.BlockSpec(memory_space=pl.ANY)
VM = pl.BlockSpec(memory_space=pltpu.VMEM)
SM = pl.BlockSpec(memory_space=pltpu.SMEM)


def sds(shape, dtype):
    return jax.ShapeDtypeStruct(shape, dtype)


def dot(a, b, ca=1, cb=0):
    return lax.dot_general(a, b, (((ca,), (cb,)), ((), ())), preferred_element_type=f32)


def params(mib):
    return pltpu.CompilerParams(vmem_limit_bytes=mib * MIB)


def cost(flops, bytes_accessed):
    return pl.CostEstimate(flops=flops, bytes_accessed=bytes_accessed, transcendentals=0)


def dma_sems(count):
    return pltpu.SemaphoreType.DMA((count,))


class Box:
    def __init__(self, names=(), refs=()):
        for n, r in zip(names, refs):
            setattr(self, n, r)

    def __getattr__(self, name):
        return None


def names_of(*tables):
    return [n for t in tables for n in t]


def shapes_of(*tables):
    return [sds(*e) for t in tables for e in t.values()]


def scratch_of(*tables, without=()):
    merged = {n: e for t in reversed(tables) for n, e in t.items() if n not in without}
    return list(merged), [pltpu.VMEM(*e) for e in merged.values()]


class Copies:
    def __init__(self, sems):
        self.sems, self.pending = sems, []

    def put(self, src, dst):
        if dst is not None:
            c = pltpu.make_async_copy(src, dst, self.sems.at[len(self.pending)])
            c.start()
            self.pending.append(c)

    def wait(self):
        for c in self.pending:
            c.wait()


def load(sems, now=4, **pairs):
    loads, copies = Box(), []
    for i, (name, (src, dst)) in enumerate(pairs.items()):
        copies.append(pltpu.make_async_copy(src, dst, sems.at[i]))
        setattr(loads, name, copies[-1])

    def start(some):
        for c in some:
            c.start()

    start(copies[:now])
    loads.later = lambda: start(copies[now:])
    return loads


def arrived(*copies):
    for c in copies:
        if c is not None:
            c.wait()


def live_rows(length, rows, cols, start=0):
    return lax.broadcasted_iota(jnp.int32, (rows, cols), 0) + start < length


def column_sum(v):
    return jnp.sum(v, axis=0, keepdims=True)


def gelu_and_slope(h):
    phi = 0.5 + 0.5 * lax.erf(h * 0.7071067811865476)
    return h * phi, phi + h * (jnp.exp(-0.5 * (h * h)) * 0.3989422804014327)


def qkv_step(x, wqkv, ab, qkv_t, loads):
    for j, ready in enumerate((loads.wq, loads.wk, loads.wv)):
        arrived(ready)
        if j == 0 and loads.later is not None:
            loads.later()
        part = dot(x[...], wqkv[:, j * D : (j + 1) * D])
        if j == 0:
            part = part + ab[0:1, :].astype(f32)
        elif j == 2:
            part = part + ab[1:2, :].astype(f32)
        low = part.astype(bf16)
        if j == 0:
            low = low * jnp.bfloat16(0.125)
        qkv_t[j * D : (j + 1) * D, :] = low.T


def head_rows(part, h):
    return slice(part * D + h * HEAD_DIM, part * D + (h + 1) * HEAD_DIM)


def attention_step(length, qkv_t, scores, expo, inv, ctx_t):
    dead_keys = lax.broadcasted_iota(jnp.int32, (16, SEQ), 1) >= length
    first_row = lax.broadcasted_iota(jnp.int32, (16, SEQ), 0) == 0
    mask_row = jnp.where(dead_keys & first_row, masked_score, 0.0).astype(bf16)
    one_row = jnp.where(first_row, 1.0, 0.0).astype(bf16)

    def score(h):
        k = jnp.concatenate([qkv_t[head_rows(1, h), :], mask_row], axis=0)
        q = jnp.concatenate([qkv_t[head_rows(0, h), :], one_row], axis=0)
        scores[h % 2] = dot(k, q, 0, 0)

    def context(h):
        c = dot(qkv_t[head_rows(2, h), :], expo[h]) * inv[h : h + 1, :]
        ctx_t[head_rows(0, h), :] = c.astype(bf16)

    score(0)
    for h in range(HEADS):
        if h + 1 < HEADS:
            score(h + 1)
        if h > 0:
            context(h - 1)
        for b in range(SEQ // RB):
            cols = slice(b * RB, (b + 1) * RB)
            s = scores[h % 2, :, cols]
            e = jnp.exp(s - jnp.max(s, axis=0, keepdims=True))
            inv[h : h + 1, cols] = 1.0 / column_sum(e)
            expo[h, :, cols] = e.astype(bf16)
    context(HEADS - 1)


def norm_rows(summed):
    centred = summed - jnp.mean(summed, axis=-1, keepdims=True)
    rstd = lax.rsqrt(jnp.mean(centred * centred, axis=-1, keepdims=True) + norm_eps)
    return centred * rstd, rstd


def first_norm_step(x, ctx_t, wout, ab, ng, ns, xh1, r1, first, nlow):
    for b in range(SEQ // RB):
        rows = slice(b * RB, (b + 1) * RB)
        summed = x[rows, :].astype(f32) + dot(ctx_t[:, rows].T, wout[...]) + ab[2:3, :].astype(f32)
        xh, rstd = norm_rows(summed)
        xh1[rows, :] = xh
        r1[rows, :] = jnp.broadcast_to(rstd, (RB, 128))
        one = xh * ng[0:1, :].astype(f32) + ns[0:1, :].astype(f32)
        first[rows, :] = one
        nlow[rows, :] = one.astype(bf16)


def feed_forward_step(nlow, win, wback, ib, hidden, act, slope, acc):
    count = FF // FT

    def into(f):
        cols = slice(f * FT, (f + 1) * FT)
        hidden[f % 2] = dot(nlow[...], win[:, cols]) + ib[:, cols].astype(f32)

    into(0)
    for f in range(count):
        cols = slice(f * FT, (f + 1) * FT)
        if f + 1 < count:
            into(f + 1)
        a, g = gelu_and_slope(hidden[f % 2])
        act[:, cols] = a.astype(bf16)
        if slope is not None:
            slope[:, cols] = g.astype(bf16)
    acc[...] = dot(act[...], wback[...])


def second_norm_step(length, first, acc, bb, ng, ns, xh2, r2, out, leave):
    for b in range(SEQ // RB):
        rows = slice(b * RB, (b + 1) * RB)
        xh, rstd = norm_rows(first[rows, :] + acc[rows, :] + bb[...].astype(f32))
        xh2[rows, :] = xh
        r2[rows, :] = jnp.broadcast_to(rstd, (RB, 128))
        y = xh * ng[1:2, :].astype(f32) + ns[1:2, :].astype(f32)
        out[rows, :] = jnp.where(live_rows(length, RB, D, b * RB), y, 0.0).astype(bf16)
        leave(pl.ds(b * RB, RB))


def norm_back(d, xh, rstd, gain):
    gd = d * gain.astype(f32)
    m1 = jnp.mean(gd, axis=-1, keepdims=True)
    m2 = jnp.mean(gd * xh, axis=-1, keepdims=True)
    return (gd - m1 - xh * m2) * rstd


def second_norm_back_step(length, d_rows, scale, xh2, r2, ng, acc, dmixed, small):
    small[...] = jnp.zeros((16, D), f32)
    for b in range(SEQ // RB):
        rows = slice(b * RB, (b + 1) * RB)
        dy = jnp.where(live_rows(length, RB, D, b * RB), d_rows[rows, :].astype(f32) * scale, 0.0)
        xh = xh2[rows, :]
        small[1:2, :] += column_sum(dy * xh)
        small[3:4, :] += column_sum(dy)
        d2 = norm_back(dy, xh, r2[rows, 0:1], ng[1:2, :])
        acc[rows, :] = d2
        low = d2.astype(bf16)
        dmixed[rows, :] = low
        small[4:5, :] += column_sum(low.astype(f32))


def feed_back_step(dmixed, wback, win, slope, dh, acc, small, arrive, leave):
    for f in range(FF // FT):
        cols = slice(f * FT, (f + 1) * FT)
        arrive(f)
        low = (dot(dmixed[...], wback[cols, :], 1, 1) * slope[:, cols].astype(f32)).astype(bf16)
        dh[:, cols] = low
        sums = column_sum(low.astype(f32))
        for piece in range(0, FT, RB):
            at = f * FT + piece
            small[8 + at // D : 9 + at // D, at % D : at % D + RB] = sums[:, piece : piece + RB]
    leave()
    acc[...] += dot(dh[...], win[...], 1, 1)


def first_norm_back_step(acc, xh1, r1, ng, dsum, dbranch, small):
    for b in range(SEQ // RB):
        rows = slice(b * RB, (b + 1) * RB)
        df = acc[rows, :]
        xh = xh1[rows, :]
        small[0:1, :] += column_sum(df * xh)
        small[2:3, :] += column_sum(df)
        d1 = norm_back(df, xh, r1[rows, 0:1], ng[0:1, :])
        dsum[rows, :] = d1
        low = d1.astype(bf16)
        dbranch[rows, :] = low
        small[5:6, :] += column_sum(low.astype(f32))


def context_back_step(wout, dbranch, dctx_t):
    dctx_t[...] = dot(wout[...], dbranch[...], 1, 1).astype(bf16)


def attention_back_step(heads, qkv_t, expo, inv, ctx_t, dctx_t, dprob, dqkv_t, arrive=lambda h: None):
    kept = {}

    def into(h):
        d_o = dctx_t[head_rows(0, h), :].astype(f32) * inv[h : h + 1, :]
        delta = column_sum(d_o * ctx_t[head_rows(0, h), :].astype(f32))
        low = d_o.astype(bf16)
        dprob[h % 2] = dot(qkv_t[head_rows(2, h), :], low, 0, 0)
        kept[h] = (low, delta)

    def out_of(h):
        low, delta = kept.pop(h)
        arrive(h)
        p = expo[h]
        ds = (p.astype(f32) * (dprob[h % 2] - delta)).astype(bf16)
        d_q = (dot(qkv_t[head_rows(1, h), :], ds) * 0.125).astype(bf16)
        d_k = dot(qkv_t[head_rows(0, h), :], ds, 1, 1).astype(bf16)
        dqkv_t[head_rows(0, h), :] = d_q
        dqkv_t[head_rows(1, h), :] = d_k
        dqkv_t[head_rows(2, h), :] = dot(low, p, 1, 1).astype(bf16)

    heads = list(heads)
    into(heads[0])
    for i, h in enumerate(heads):
        if i + 1 < len(heads):
            into(heads[i + 1])
        out_of(h)


def qkv_back_step(dqkv_t, dqkv, small):
    for j in range(3):
        low = dqkv_t[j * D : (j + 1) * D, :].T
        dqkv[:, j * D : (j + 1) * D] = low
        if j != 1:
            at = 6 + j // 2
            small[at : at + 1, :] = column_sum(low.astype(f32))


def input_back_step(dqkv, wqkv, dsum, din, leave=lambda rows: None):
    for b in range(SEQ // RB):
        rows = slice(b * RB, (b + 1) * RB)
        din[rows, :] = (dot(dqkv[rows, :], wqkv[...], 1, 1) + dsum[rows, :]).astype(bf16)
        leave(pl.ds(b * RB, RB))


ROWS16 = ((SEQ, D), bf16)
ROWS32 = ((SEQ, D), f32)
COLS16 = ((D, SEQ), bf16)
STD = ((SEQ, 128), f32)
WIDE16 = ((SEQ, FF), bf16)
QKV_T = ((3 * D, SEQ), bf16)
EXPO = ((HEADS, SEQ, SEQ), bf16)
INV = ((16, SEQ), f32)
SCORES = ((2, SEQ, SEQ), f32)
SMALL = ((16, D), f32)
HALF = ((SEQ, D // 2), bf16)
HALF_T = ((D // 2, SEQ), bf16)

OUT = dict(out=ROWS16)
SHARED = dict(
    x_own=HALF, x_send=HALF, ctx_own=HALF_T, ctx_send=HALF_T, nlow=ROWS16, act_own=((SEQ, FF // 2), bf16),
    act_send=((SEQ, FF // 2), bf16),
)
STORED = dict(
    qkv_t=QKV_T, expo=EXPO, inv=INV, ctx_t=COLS16, xh1=ROWS32, r1=STD, slope=WIDE16, xh2=ROWS32, r2=STD
)
NORM_OUTS = dict(dmixed=ROWS16)
BLOCK2 = ((2, SEQ, UNIT), bf16)
FFN_OUTS = dict(
    dh0=HALF, dh1=HALF, dh2=HALF, dh3=HALF, ds0=HALF, ds1=HALF, ds2=HALF, ds3=HALF, dbranch=ROWS16
)
ATT_OUTS = dict(
    dqkv0=BLOCK2, dqkv1=BLOCK2, dqkv2=BLOCK2, small=SMALL
)
DIN = dict(din=ROWS16)
NORM_MORE = dict(acc=ROWS32, small=SMALL)
FFN_MORE = dict(dctx_t=COLS16, dsum=ROWS32, small=SMALL)

WEIGHTS = dict(wqkv=((D, 3 * D), bf16), wout=((D, D), bf16), win=((D, FF), bf16), wback=((FF, D), bf16))
FORWARD = dict(
    x=ROWS16, qkv_t=QKV_T, scores=SCORES, expo=EXPO, inv=INV, ctx_t=COLS16, nlow=ROWS16, xh1=ROWS32, r1=STD,
    first=ROWS32, act=WIDE16, slope=WIDE16, xh2=ROWS32, r2=STD, out=ROWS16, acc=ROWS32,
)
BACK_FFN = dict(
    acc=ROWS32, dmixed=ROWS16, dh=WIDE16, dsum=ROWS32, dbranch=ROWS16, dctx_t=COLS16, small=SMALL
)
BACK_ATT = dict(dqkv_t=QKV_T, dqkv=((SEQ, 3 * D), bf16), din=ROWS16)


def halves(core, width):
    return (
        pl.ds(pl.multiple_of(core * width, 128), width),
        pl.ds(pl.multiple_of((1 - core) * width, 128), width),
    )


def weight_loads(v, wqkv, wout, win, wback):
    parts = [pl.ds(j * D, D) for j in range(3)]
    wq, wk, wv = [(wqkv.at[:, p], v.wqkv.at[:, p]) for p in parts]
    return dict(wq=wq, wk=wk, wv=wv, wout=(wout, v.wout), win=(win, v.win), wback=(wback, v.wback))


def forward_steps(v, w, o, length, core, copies, loads):
    own_d, other_d = halves(core, D // 2)
    own_f, other_f = halves(core, FF // 2)
    arrived(loads.x)
    copies.put(v.x.at[:, own_d], o.x_own)
    copies.put(v.x.at[:, other_d], o.x_send)
    qkv_step(v.x, v.wqkv, w.ab, v.qkv_t, loads)
    copies.put(v.qkv_t, o.qkv_t)
    attention_step(length, v.qkv_t, v.scores, v.expo, v.inv, v.ctx_t)
    copies.put(v.ctx_t.at[own_d, :], o.ctx_own)
    copies.put(v.ctx_t.at[other_d, :], o.ctx_send)
    copies.put(v.expo, o.expo)
    copies.put(v.inv, o.inv)
    copies.put(v.ctx_t, o.ctx_t)
    arrived(loads.wout)
    first_norm_step(v.x, v.ctx_t, v.wout, w.ab, w.ng, w.ns, v.xh1, v.r1, v.first, v.nlow)
    copies.put(v.nlow, o.nlow)
    copies.put(v.xh1, o.xh1)
    copies.put(v.r1, o.r1)
    arrived(loads.win, loads.wback)
    feed_forward_step(v.nlow, v.win, v.wback, w.ib, v.scores, v.act, v.slope, v.acc)
    copies.put(v.act.at[:, own_f], o.act_own)
    copies.put(v.act.at[:, other_f], o.act_send)
    copies.put(v.slope, o.slope)

    def leave(rows):
        if o.out is not None:
            copies.put(v.out.at[rows, :], o.out.at[rows, :])

    second_norm_step(length, v.first, v.acc, w.bb, w.ng, w.ns, v.xh2, v.r2, v.out, leave)
    copies.put(v.xh2, o.xh2)
    copies.put(v.r2, o.r2)


def leave_hidden(dh, o, core, copies):
    for refs, c in (((o.ds0, o.ds1, o.ds2, o.ds3), 1 - core), ((o.dh0, o.dh1, o.dh2, o.dh3), core)):
        for i, ref in enumerate(refs):
            half, block = i // 2, i % 2
            at = pl.multiple_of(half * (FF // 2) + c * (FF // 4) + block * UNIT, 128)
            copies.put(dh.at[:, pl.ds(at, UNIT)], ref)


def ffn_back_steps(v, w, o, core, copies):
    def leave():
        leave_hidden(v.dh, o, core, copies)

    feed_back_step(v.dmixed, v.wback, v.win, v.slope, v.dh, v.acc, v.small, lambda f: None, leave)
    first_norm_back_step(v.acc, v.xh1, v.r1, w.ng, v.dsum, v.dbranch, v.small)
    copies.put(v.dbranch, o.dbranch)
    context_back_step(v.wout, v.dbranch, v.dctx_t)


def leave_dqkv(v, o, copies):
    for u, ref in enumerate((o.dqkv0, o.dqkv1, o.dqkv2)):
        for half in range(2):
            copies.put(v.dqkv.at[:, pl.ds((3 * half + u) * UNIT, UNIT)], ref.at[half])
    copies.put(v.small, o.small)


def attention_back_end(v, o, copies):
    qkv_back_step(v.dqkv_t, v.dqkv, v.small)
    leave_dqkv(v, o, copies)
    input_back_step(
        v.dqkv, v.wqkv, v.dsum, v.din, lambda rows: copies.put(v.din.at[rows, :], o.din.at[rows, :])
    )


SMALL_WEIGHTS = dict(ab=0, ng=0, ns=0, ib=0, bb=0)


def here(lengths):
    z, core, shard = lax.axis_index(Z), lax.axis_index(CORE), lax.axis_index(SHARD)
    read = (z * 2 + core) * lax.axis_size(SHARD) + shard
    return jnp.where(lax.axis_index(SECTION) == 0, 1, 0), lengths[read], core


def first_kernel(names, out_names, lengths, x, wqkv, wout, win, wback, ab, ng, ns, ib, bb, *rest):
    n = len(out_names)
    o = Box(out_names, rest[:n])
    v = Box(names, rest[n:-2])
    w = Box(SMALL_WEIGHTS, (ab, ng, ns, ib, bb))
    live, length, core = here(lengths)

    @pl.when(live == 1)
    def _():
        loads = load(rest[-2], x=(x, v.x), **weight_loads(v, wqkv, wout, win, wback))
        copies = Copies(rest[-1])
        forward_steps(v, w, o, length, core, copies, loads)
        copies.wait()


def first_forward(lengths, x, weights, tables, name):
    without = () if STORED in tables else ("slope",)
    names, scratch = scratch_of(WEIGHTS, FORWARD, without=without)
    outs = shapes_of(*tables)
    return pl.pallas_call(
        partial(first_kernel, names, names_of(*tables)),
        out_shape=outs,
        in_specs=[SM, ANY] + [HBM] * 4 + [VM] * 5,
        out_specs=[HBM] * len(outs),
        scratch_shapes=scratch + [dma_sems(7), dma_sems(len(outs) + 1)],
        compiler_params=params(54),
        cost_estimate=cost(8 * 10**9, 36 * 10**6),
        name=name,
    )(lengths, x, *weights)


SECOND_OUTS = (OUT, SHARED, NORM_OUTS, FFN_OUTS, ATT_OUTS, DIN)


def second_kernel(names, scal, scale, x, cot, wqkv, wout, win, wback, ab, ng, ns, ib, bb, *rest):
    rest = rest[1 + len(SHARED) :]
    out_names = names_of(*SECOND_OUTS)
    n = len(out_names)
    o = Box(out_names, rest[:n])
    v = Box(names, rest[n:-2])
    w = Box(SMALL_WEIGHTS, (ab, ng, ns, ib, bb))

    @pl.when(scal[0] == 1)
    def _():
        length, core = scal[1], scal[2]
        loads = load(rest[-2], x=(x, v.x), **weight_loads(v, wqkv, wout, win, wback), cot=(cot, v.cot))
        copies = Copies(rest[-1])
        v.dsum, v.dh, v.dqkv_t = v.first, v.slope, v.qkv_t
        forward_steps(v, w, o, length, core, copies, loads)
        arrived(loads.cot)
        second_norm_back_step(length, v.cot, scale[0], v.xh2, v.r2, w.ng, v.acc, v.dmixed, v.small)
        copies.put(v.dmixed, o.dmixed)
        ffn_back_steps(v, w, o, core, copies)
        attention_back_step(range(HEADS), v.qkv_t, v.expo, v.inv, v.ctx_t, v.dctx_t, v.scores, v.dqkv_t)
        attention_back_end(v, o, copies)
        copies.wait()


def second_layer(scal, scale, x, cot, weights, shared):
    names, scratch = scratch_of(
        WEIGHTS, FORWARD, BACK_FFN, BACK_ATT, dict(cot=ROWS16), without=("dsum", "dh", "dqkv_t")
    )
    outs = shapes_of(*SECOND_OUTS)
    n_in = 13
    flat = pl.pallas_call(
        partial(second_kernel, names),
        out_shape=outs,
        in_specs=[SM, SM, ANY, ANY] + [HBM] * 4 + [VM] * 5 + [HBM] * len(shared),
        out_specs=[HBM] * len(outs),
        input_output_aliases={n_in + i: i for i in range(len(shared))},
        scratch_shapes=scratch + [dma_sems(8), dma_sems(len(outs) + 7)],
        compiler_params=params(57),
        cost_estimate=cost(20 * 10**9, 36 * 10**6),
        name="second_layer",
    )(scal, scale, x, cot, *weights, *shared)
    return Box(names_of(*SECOND_OUTS), flat)


def pick(source, table):
    return [getattr(source, n) for n in table]


def in_hbm(arrays):
    return [pltpu.with_memory_space_constraint(a, pltpu.HBM) for a in arrays]


def take_late(pairs, sems):
    copies = Copies(sems)
    for src, dst in pairs:
        copies.put(src, dst)
    copies.wait()


def norm_back_kernel(scal, d_rows, xh2, r2, ng, late, dmixed, acc, small, sems):
    @pl.when(scal[0] == 1)
    def _():
        second_norm_back_step(scal[1], d_rows, 1.0, xh2, r2, ng, acc, dmixed, small)

    @pl.when(scal[0] == 0)
    def _():
        take_late([(late, dmixed)], sems)


def first_norm_back(scal, d_rows, given, late):
    outs = shapes_of(NORM_OUTS, NORM_MORE)
    flat = pl.pallas_call(
        norm_back_kernel,
        out_shape=outs,
        in_specs=[SM, VM, VM, VM, VM, HBM],
        out_specs=[VM] * len(outs),
        scratch_shapes=[dma_sems(1)],
        compiler_params=params(8),
        cost_estimate=cost(2 * 10**10, 6 * 10**6),
        name="first_norm_back",
    )(scal, d_rows, given.xh2, given.r2, given.ng, *in_hbm([late.dmixed]))
    return flat[0], Box(NORM_MORE, flat[1:])


FFN_LOADS = dict(dmixed=0, wback=0, slope=0, win=0, acc=0, small=0, xh1=0, r1=0, wout=0, ng=0)


def ffn_back_kernel(scal, *rest):
    given = Box(FFN_LOADS, rest)
    rest = rest[len(FFN_LOADS) :]
    late = rest[: len(FFN_OUTS)]
    rest = rest[len(FFN_OUTS) :]
    o = Box(names_of(FFN_OUTS, FFN_MORE), rest)
    dh, acc, sems = rest[-3:]

    @pl.when(scal[0] == 1)
    def _():
        core = scal[2]
        copies = Copies(sems)
        acc[...] = given.acc[...]
        o.small[...] = given.small[...]

        def leave():
            leave_hidden(dh, o, core, copies)

        feed_back_step(given.dmixed, given.wback, given.win, given.slope, dh, acc, o.small, lambda f: None, leave)
        first_norm_back_step(acc, given.xh1, given.r1, given.ng, o.dsum, o.dbranch, o.small)
        context_back_step(given.wout, o.dbranch, o.dctx_t)
        copies.wait()

    @pl.when(scal[0] == 0)
    def _():
        take_late(zip(late, pick(o, FFN_OUTS)), sems)


def first_ffn_back(scal, given, late):
    outs = shapes_of(FFN_OUTS, FFN_MORE)
    flat = pl.pallas_call(
        ffn_back_kernel,
        out_shape=outs,
        in_specs=[SM] + [VM] * len(FFN_LOADS) + [HBM] * len(FFN_OUTS),
        out_specs=[VM] * len(outs),
        scratch_shapes=[pltpu.VMEM(*WIDE16), pltpu.VMEM(*ROWS32), dma_sems(len(FFN_OUTS))],
        compiler_params=params(14),
        cost_estimate=cost(6 * 10**9, 25 * 10**6),
        name="first_ffn_back",
    )(scal, *pick(given, FFN_LOADS), *in_hbm(pick(late, FFN_OUTS)))
    n = len(FFN_OUTS)
    return Box(FFN_OUTS, flat), Box(FFN_MORE, flat[n:])


ATT_FIRST = dict(qkv_t=0, expo=0, inv=0, ctx_t=0, dctx_t=0)
ATT_LATER = dict(small=0)


def att_early_kernel(heads, scal, qkv_t, expo, inv, ctx_t, dctx_t, out, dqkv_t, dprob):
    @pl.when(scal[0] == 1)
    def _():
        attention_back_step(heads, qkv_t, expo, inv, ctx_t, dctx_t, dprob, dqkv_t)
        size = len(heads) * HEAD_DIM
        for p in range(3):
            low = p * D + heads[0] * HEAD_DIM
            out[p * size : (p + 1) * size, :] = dqkv_t[low : low + size, :]


def first_att_back_early(scal, heads, given):
    return pl.pallas_call(
        partial(att_early_kernel, heads),
        out_shape=sds((3 * len(heads) * HEAD_DIM, SEQ), bf16),
        in_specs=[SM] + [VM] * len(ATT_FIRST),
        out_specs=VM,
        scratch_shapes=[pltpu.VMEM(*QKV_T), pltpu.VMEM(*SCORES)],
        compiler_params=params(10),
        cost_estimate=cost(0, 0),
        name="first_att_back_early",
    )(scal, *pick(given, ATT_FIRST))


def att_end_kernel(names, heads, scal, *rest):
    given = Box(names_of(ATT_FIRST, ATT_LATER), rest)
    rest = rest[len(ATT_FIRST) + len(ATT_LATER) :]
    early, late, rest = rest[0], rest[1 : 1 + len(ATT_OUTS)], rest[1 + len(ATT_OUTS) :]
    o = Box(ATT_OUTS, rest)
    v = Box(names, rest[len(ATT_OUTS) : -1])

    @pl.when(scal[0] == 1)
    def _():
        g = given
        attention_back_step(heads, g.qkv_t, g.expo, g.inv, g.ctx_t, g.dctx_t, v.scores, v.dqkv_t)
        size = heads[0] * HEAD_DIM
        for p in range(3):
            v.dqkv_t[p * D : p * D + size, :] = early[p * size : (p + 1) * size, :]
        v.small[...] = g.small[...]
        copies = Copies(rest[-1])
        qkv_back_step(v.dqkv_t, v.dqkv, v.small)
        leave_dqkv(v, o, copies)
        copies.wait()

    @pl.when(scal[0] == 0)
    def _():
        stages = [v.dqkv.at[:, pl.ds(i * UNIT, UNIT)] for i in range(6)] + [v.small]
        before = [late[u].at[half] for u in range(3) for half in range(2)] + list(late[3:])
        there = [r.at[half] for r in (o.dqkv0, o.dqkv1, o.dqkv2) for half in range(2)] + [o.small]
        take_late(zip(before, stages), rest[-1])
        take_late(zip(stages, there), rest[-1])


def first_att_back(scal, heads, given, early, late):
    names, scratch = scratch_of(BACK_ATT, dict(scores=SCORES, small=SMALL), without=("din",))
    outs = [pltpu.HBM(*e) for e in ATT_OUTS.values()]
    flat = pl.pallas_call(
        partial(att_end_kernel, names, heads),
        out_shape=outs,
        in_specs=[SM] + [VM] * (len(ATT_FIRST) + len(ATT_LATER) + 1) + [HBM] * len(ATT_OUTS),
        out_specs=[HBM] * len(outs),
        scratch_shapes=scratch + [dma_sems(len(outs) + 3)],
        compiler_params=params(18),
        cost_estimate=cost(0, 0),
        name="first_att_back",
    )(scal, *pick(given, ATT_FIRST), *pick(given, ATT_LATER), early, *in_hbm(pick(late, ATT_OUTS)))
    return Box(ATT_OUTS, flat)


def input_back_kernel(scal, d0, d1, d2, wqkv, dsum, late, din, dqkv, w, ds, stage, sems):
    @pl.when(scal[0] == 1)
    def _():
        copies = Copies(sems)
        for u, ref in enumerate((d0, d1, d2)):
            for half in range(2):
                copies.put(ref.at[half], dqkv.at[:, pl.ds((3 * half + u) * UNIT, UNIT)])
        copies.put(wqkv, w)
        copies.put(dsum, ds)
        copies.wait()
        input_back_step(dqkv, w, ds, stage)

    @pl.when(scal[0] == 0)
    def _():
        take_late([(late, stage)], sems)

    take_late([(stage, din)], sems)


def first_input_back(scal, dqkv, wqkv, dsum, late):
    return pl.pallas_call(
        input_back_kernel,
        out_shape=pltpu.HBM(*ROWS16),
        in_specs=[SM] + [HBM] * 6,
        out_specs=HBM,
        scratch_shapes=[
            pltpu.VMEM((SEQ, 3 * D), bf16), pltpu.VMEM(*WEIGHTS["wqkv"]), pltpu.VMEM(*ROWS32), pltpu.VMEM(*ROWS16),
            dma_sems(8),
        ],
        compiler_params=params(16),
        cost_estimate=cost(0, 0),
        name="first_input_back",
    )(scal, *in_hbm(dqkv), *in_hbm([wqkv, dsum, late]))


def half_of_small(small, h):
    rows = [small[0:8, h * UNIT : (h + 1) * UNIT]]
    for j in range(4):
        at = h * (FF // 2) + j * UNIT
        rows.append(small[8 + at // D : 9 + at // D, at % D : at % D + UNIT])
    rows.append(jnp.zeros((4, UNIT), f32))
    return jnp.concatenate(rows, axis=0)


def grad_kernel(pieces, n_in, scal, *refs):
    ins, outs = refs[:n_in], refs[n_in:]
    keep_at = scal[3]
    for out, half in zip(outs, (1 - keep_at, keep_at)):
        at = 0
        for a1, a2, a_dim, a_start, a_size, b1, b2, b_start in pieces:
            block = slice(a_start, a_start + a_size)

            def left(i):
                return ins[i][:, block] if a_dim == 0 else ins[i][block, :]

            def right(i):
                if isinstance(i, tuple):
                    return jnp.where(half == 0, ins[i[0]][...], ins[i[1]][...])
                width = ins[i].shape[1] // 2
                return ins[i][:, pl.ds(pl.multiple_of(half * width + b_start, 128), UNIT)]

            total = dot(left(a1), right(b1), a_dim, 0) + dot(left(a2), right(b2), a_dim, 0)
            out[at : at + a_size, :] = total.astype(bf16)
            at += a_size


def grad_chunk(scal, operands, pieces, name):
    rows = sum(p[4] for p in pieces)
    return pl.pallas_call(
        partial(grad_kernel, pieces, len(operands)),
        out_shape=[sds((rows, UNIT), bf16)] * 2,
        in_specs=[SM] + [VM] * len(operands),
        out_specs=[VM] * 2,
        compiler_params=params(10),
        cost_estimate=cost(2 * 10**10, 6 * 10**6),
        name=name,
    )(scal, *operands)


def last_grads_kernel(scal, *refs):
    blocks, others = refs[7:13], refs[:7]
    sides = refs[13:17]
    stages, b, sems = refs[17:24], refs[24], refs[25]
    x1, x2, c1, c2, db1, db2, small = stages
    first, units, rest = Copies(sems.at[pl.ds(0, 2)]), Copies(sems.at[pl.ds(2, 6)]), Copies(sems.at[pl.ds(8, 5)])
    for i in range(2):
        first.put(others[i], stages[i])
    for u in range(3):
        for i in range(2):
            units.put(blocks[3 * i + u], b.at[u, i])
    for i in range(2, 7):
        rest.put(others[i], stages[i])
    keep_at = scal[3]
    sides = tuple(zip((1 - keep_at, keep_at), sides[0:2], sides[2:4]))
    first.wait()
    for u in range(3):
        arrived(*units.pending[2 * u : 2 * u + 2])
        for half, *outs in sides:
            total = dot(x1[...], b[u, 0, half], 0, 0) + dot(x2[...], b[u, 1, half], 0, 0)
            outs[u // 2][u % 2 * UNIT : (u % 2 + 1) * UNIT, :] = total.astype(bf16)
    rest.wait()
    for half, _, out in sides:
        cols = pl.ds(pl.multiple_of(half * UNIT, 128), UNIT)
        out[UNIT : 2 * UNIT, :] = (dot(c1[...], db1[:, cols]) + dot(c2[...], db2[:, cols])).astype(bf16)
        out[2 * UNIT : 2 * UNIT + 16, :] = jnp.where(half == 0, half_of_small(small[...], 0), half_of_small(small[...], 1)).astype(bf16)


def last_grads(scal, others, blocks):
    stages = (HALF, HALF, HALF_T, HALF_T, ROWS16, ROWS16, SMALL)
    return pl.pallas_call(
        last_grads_kernel,
        out_shape=[sds((2 * UNIT, UNIT), bf16)] * 2 + [sds((2 * UNIT + 16, UNIT), bf16)] * 2,
        in_specs=[SM] + [ANY] * 13,
        out_specs=[VM] * 4,
        scratch_shapes=[pltpu.VMEM(*e) for e in stages]
        + [pltpu.VMEM((3, 2, 2, SEQ, UNIT), bf16), dma_sems(13)],
        compiler_params=params(18),
        cost_estimate=cost(0, 0),
        name="last_grads",
    )(scal, *others, *blocks)


def place_kernel(moves, n_prev, n_out, scal, own, other, *rest):
    outs = rest[n_prev : n_prev + n_out]
    stage, sem = rest[-2:]
    core = scal[2]
    copies = Copies(sem)
    for i, (ref, c) in enumerate(((own, core), (other, 1 - core))):
        stage[i] = ref[...].astype(f32)
        for out, src, size, rows, row_step, col, col_step in moves:
            row = pl.multiple_of(rows + c * row_step, 8)
            column = pl.multiple_of(col + c * col_step, 128)
            copies.put(stage.at[i, pl.ds(src, size), :], outs[out].at[pl.ds(row, size), pl.ds(column, UNIT)])
    if n_out < len(rest) - 2 - n_prev:
        bias, gain, shift, hidden, last = rest[n_prev + n_out : -2]
        at = own.shape[0] - 16
        small = own[at : at + 16, :].astype(f32) + other[at : at + 16, :].astype(f32)
        gain[...] = small[0:2, :]
        shift[...] = small[2:4, :]
        last[...] = small[4:5, :]
        bias[0:1, :] = small[6:7, :]
        bias[1:2, :] = small[7:8, :]
        bias[2:3, :] = small[5:6, :]
        for j in range(4):
            hidden[:, j * UNIT : (j + 1) * UNIT] = small[8 + j : 9 + j, :]
    copies.wait()


SMALL_OUTS = ((3, UNIT), (2, UNIT), (2, UNIT), (1, FF // 2), (1, UNIT))


def place(scal, own, other, moves, shapes, previous, with_small=False):
    kept = [i for i, p in enumerate(previous) if p is not None]
    small = [sds(s, f32) for s in SMALL_OUTS] if with_small else []
    return pl.pallas_call(
        partial(place_kernel, moves, len(kept), len(shapes)),
        out_shape=[sds(s, f32) for s in shapes] + small,
        in_specs=[SM, VM, VM] + [HBM] * len(kept),
        out_specs=[HBM] * len(shapes) + [VM] * len(small),
        input_output_aliases={3 + j: i for j, i in enumerate(kept)},
        scratch_shapes=[pltpu.VMEM((2,) + own.shape, f32), dma_sems(2 * len(moves))],
        compiler_params=params(8),
        cost_estimate=cost(0, own.size * 12),
        name="place",
    )(scal, own, other, *[previous[i] for i in kept])


def add_kernel(start, a, b, out):
    rows = slice(start, start + out.shape[0])
    out[...] = (a[rows, :].astype(f32) + b[rows, :].astype(f32)).astype(bf16)


def added(a, b, start=0, size=None):
    rows = slice(start, start + (a.shape[0] if size is None else size))
    return (a[rows].astype(f32) + b[rows].astype(f32)).astype(bf16)


def take_kernel(takes, a, b, out):
    @pl.when(takes[0] == 1)
    def _():
        out[...] = a[...]

    @pl.when(takes[0] == 0)
    def _():
        out[...] = b[...]


def taken(takes, a, b):
    return jnp.where(takes[0] == 1, a, b)


def read_weights(lengths, assignment):
    member = assignment == jnp.arange(MICRO, dtype=jnp.int32)[None, :]
    counts = jnp.sum(jnp.where(member, lengths[:, None], 0), axis=0)
    token_total = jnp.sum(lengths).astype(f32)
    scales = token_total / (MICRO * counts.astype(f32))
    return jnp.sum(jnp.where(member, scales[None, :], 0.0), axis=1)


class Order:
    def __init__(self):
        self.last = None

    def after(self, value):
        if self.last is not None:
            value, self.last = lax.optimization_barrier((value, self.last))
        return value

    def done(self, value):
        self.last = value
        return value


class Sums:
    def __init__(self, scal, order, z_index, z_count, shapes):
        self.scal, self.order, self.z_index, self.z_count, self.shapes = scal, order, z_index, z_count, shapes
        self.value, self.moving, self.keep, self.results, self.small = {}, {}, {}, {}, None
        half = z_count // 2
        self.stages = [[self.shard_done, partial(self.inward, hop=0)]]
        for hop in range(half - 1):
            self.stages.append([self.add, self.middle if hop + 2 == half else partial(self.inward, hop=hop + 1)])
        self.stages.append([self.add, partial(self.outward, hop=half - 2)])
        for hop in range(half - 2, -1, -1):
            after = partial(self.outward, hop=hop - 1) if hop > 0 else self.core
            self.stages.append([partial(self.take, hop=hop), after])
        self.stages.append([self.place])

    def start(self, pair, sizes):
        moving, at = lax.ppermute(pair[0], SHARD, SWAP), 0
        for size in sizes:
            i = len(self.keep)
            self.keep[i], self.moving[i] = pair[1], (moving, at, size)
            at += size

    def tick(self, t):
        for stage in (4, 3) if t == len(PLACES) + 2 else range(5):
            for i in range(len(PLACES)):
                if t == i + stage - (stage == 0 and i > 3):
                    for step in self.stages[stage]:
                        step(i)

    def shard_done(self, i):
        moving, at, size = self.moving[i]
        self.value[i] = self.order.done(added(self.order.after(moving), self.keep[i], at, size))

    def inward(self, i, hop):
        last = self.z_count - 1
        self.moving[i] = lax.ppermute(self.value[i], Z, [(hop, hop + 1), (last - hop, last - 1 - hop)])

    def add(self, i):
        self.value[i] = self.order.done(added(self.value[i], self.order.after(self.moving[i])))

    def middle(self, i):
        half = self.z_count // 2
        self.moving[i] = lax.ppermute(self.value[i], Z, [(half - 1, half), (half, half - 1)])

    def outward(self, i, hop):
        last = self.z_count - 1
        self.moving[i] = lax.ppermute(self.value[i], Z, [(hop + 1, hop), (last - 1 - hop, last - hop)])

    def take(self, i, hop):
        takes = ((self.z_index == hop) | (self.z_index == self.z_count - 1 - hop)).astype(jnp.int32)[None]
        self.value[i] = self.order.done(taken(takes, self.order.after(self.moving[i]), self.value[i]))

    def core(self, i):
        self.moving[i] = lax.ppermute(self.value[i], CORE, SWAP)

    def place(self, i):
        targets, moves, with_small = PLACES[i]
        flat = place(
            self.scal, self.value[i], self.order.after(self.moving[i]), moves, [self.shapes[t] for t in targets],
            [self.results.get(t) for t in targets], with_small,
        )
        self.order.done(flat[0])
        for t, r in zip(targets, flat):
            self.results[t] = r
        if with_small:
            self.small = flat[len(targets) :]


G_BACK, G_IN, G_QKV, G_OUT = range(4)
PLACES = (
    ((G_BACK,), ((0, 0, D, 0, FF // 2, 0, 0),), False),
    ((G_BACK,), ((0, 0, D, D, FF // 2, 0, 0),), False),
    ((G_IN,), ((0, 0, D, 0, 0, 0, FF // 4),), False),
    ((G_IN,), ((0, 0, D, 0, 0, UNIT, FF // 4),), False),
    ((G_QKV,), ((0, 0, UNIT, 0, UNIT, 0, 0), (0, UNIT, UNIT, 0, UNIT, UNIT, 0)), False),
    ((G_QKV, G_OUT), ((0, 0, UNIT, 0, UNIT, 2 * UNIT, 0), (1, UNIT, UNIT, 0, UNIT, 0, 0)), True),
)


def sums_by_collectives(pairs, small, shard, shard_count):
    side = [[p[1] for p in pairs], [p[0] for p in pairs]]
    back = jnp.concatenate([jnp.concatenate(s[0:2], axis=0) for s in side], axis=1)
    inner = jnp.stack([jnp.concatenate([s[2][:D], s[2][D:]], axis=1) for s in side], axis=1)
    qkv = jnp.concatenate([part for s in side for part in (s[3][:UNIT], s[3][UNIT:], s[4][:UNIT])], axis=1)
    out = jnp.concatenate([s[4][UNIT : 2 * UNIT] for s in side], axis=1)

    def mine(whole):
        width = whole.shape[1] // shard_count
        return lax.dynamic_slice_in_dim(whole, shard * width, width, 1)

    def by_rows(quarter):
        return mine(lax.all_gather(lax.psum(quarter.astype(f32), (Z, SHARD)), CORE, axis=0, tiled=True))

    inner = lax.all_gather(lax.psum(inner.astype(f32), (Z, SHARD)), CORE, axis=2).reshape(D, FF)
    total = lax.psum(small, DATA)
    part = mine(total)
    hidden = mine(total[8:12].reshape(1, FF))
    results = {G_BACK: by_rows(back), G_IN: mine(inner), G_QKV: by_rows(qkv), G_OUT: by_rows(out)}
    return results, (jnp.stack([part[6], part[7], part[5]]), part[0:2], part[2:4], hidden, part[4:5])


def body(
    block_input, cotangent, lengths, assignment, qkv_weight, out_weight, in_weight, back_weight, attn_bias, norm_gain,
    norm_shift, in_bias, back_bias,
):
    section = lax.axis_index(SECTION)
    z_index, core, shard = lax.axis_index(Z), lax.axis_index(CORE), lax.axis_index(SHARD)
    z_count, shard_count = lax.axis_size(Z), lax.axis_size(SHARD)
    weights = (
        qkv_weight[0], out_weight[0], in_weight[0], back_weight[0], attn_bias[0], norm_gain[0], norm_shift[0], in_bias,
        back_bias,
    )
    keep_at = shard if shard_count == 2 else 0
    (out,) = first_forward(lengths, block_input, weights, (OUT,), "first_forward")
    received = lax.ppermute(out, SECTION, [(0, 1)])
    lengths, assignment, _ = lax.optimization_barrier((lengths, assignment, out))
    data_index = (z_index * 2 + core) * shard_count + shard
    length = lax.dynamic_index_in_dim(lengths, data_index, 0, keepdims=False)
    own_scale = lax.dynamic_slice_in_dim(read_weights(lengths, assignment), data_index, 1)

    def scalars(live):
        return jnp.stack([live.astype(jnp.int32), length, core, jnp.asarray(keep_at, jnp.int32)])

    def core_swap(array):
        return lax.ppermute(array, CORE, SWAP)

    at_first, at_second = scalars(section == 0), scalars(section == 1)
    kept = first_forward(lengths, block_input, weights, (SHARED, STORED), "first_forward_kept")
    given = Box(names_of(SHARED, STORED), kept)
    late = second_layer(at_second, own_scale, *in_hbm([received]), cotangent, weights, [out, *kept[: len(SHARED)]])
    returned = lax.ppermute(late.din, SECTION, [(1, 0)])
    from_peer = [core_swap(a) for a in (late.act_send, late.nlow, late.x_send, late.ctx_send)]
    returned, from_peer = lax.optimization_barrier((returned, from_peer))
    act_peer, nlow_peer, x_peer, ctx_peer = from_peer

    order = Order()
    shapes = {
        G_QKV: (D, 3 * D // shard_count), G_OUT: (D, D // shard_count), G_IN: (D, FF // shard_count),
        G_BACK: (FF, D // shard_count),
    }
    sums = Sums(at_first, order, z_index, z_count, shapes)
    pairs = []

    def start(pair, sizes):
        pairs.append(pair)
        if shard_count == 2:
            sums.start(pair, sizes)

    def grad(operands, pieces, name):
        pair = grad_chunk(order.after(at_first), operands, pieces, name)
        order.done(pair[0])
        start(pair, (D,) * len(pieces))

    def tick(*args):
        if shard_count == 2:
            sums.tick(*args)

    given.ng, given.wqkv, given.wout, given.win, given.wback = norm_gain[0], *weights[:4]
    given.dmixed, more = first_norm_back(at_first, returned, given, late)
    given.acc, given.small = more.acc, more.small
    dmixed_peer = core_swap(given.dmixed)
    for k in range(2):
        grad((late.act_own, act_peer, given.dmixed, dmixed_peer), ((0, 1, 0, k * D, D, 2, 3, 0),), "grad_back")
    ffn, more = first_ffn_back(order.after(at_first), given, late)
    order.done(ffn.dbranch)
    given.dctx_t, given.dsum, given.small = more.dctx_t, more.dsum, more.small
    own = (ffn.dh0, ffn.dh1, ffn.dh2, ffn.dh3)
    peer = [core_swap(a) for a in (ffn.ds0, ffn.ds1, ffn.ds2, ffn.ds3)]
    tick(0)
    operands = (late.nlow, nlow_peer, *own, *peer)
    grad(operands, ((0, 1, 0, 0, D, (2, 4), (6, 8), 0), (0, 1, 0, 0, D, (3, 5), (7, 9), 0)), "grad_in")
    dbranch_peer = core_swap(ffn.dbranch)
    cut = HEADS - 2
    early = order.done(first_att_back_early(order.after(at_first), range(cut), given))
    tick(1)
    go, dbranch_peer = order.after((at_first, dbranch_peer))
    att = first_att_back(go, range(cut, HEADS), given, early, late)
    order.done(att.small)
    own = (att.dqkv0, att.dqkv1, att.dqkv2)
    peer = [core_swap(a) for a in own]

    x_own, ctx_own, x_peer, ctx_peer, small = in_hbm([late.x_own, late.ctx_own, x_peer, ctx_peer, att.small])
    others = (x_own, x_peer, ctx_own, ctx_peer, ffn.dbranch, dbranch_peer, small)
    last = last_grads(order.after(at_first), others, (*in_hbm(own), *peer))
    order.done(last[0])
    start(last[0:2], (D,))
    start(last[2:4], (D + 16,))
    if shard_count == 2:
        for t in range(2, len(PLACES) + len(sums.stages) - 1):
            tick(t)
            if t == 7:
                din = order.done(first_input_back(order.after(at_first), own, weights[0], given.dsum, late.din))
        results, small = sums.results, sums.small
    else:
        din = first_input_back(at_first, own, weights[0], given.dsum, late.din)
        results, small = sums_by_collectives(pairs, att.small, shard, shard_count)
    return (
        late.out[None], din[None], results[G_QKV][None], results[G_OUT][None], results[G_IN][None],
        results[G_BACK][None], small[0][None], small[1][None], small[2][None], small[3], small[4],
    )


def solution(mesh):
    sections, groups, shards = mesh.devices.shape
    mesh = Mesh(mesh.devices.reshape(sections, groups // 2, 2, shards), (SECTION, Z, CORE, SHARD))
    rows, layers, pairs = P(DATA, None), P(SECTION, None, None), P(SECTION, None)
    both, columns = P(SECTION, DATA, None), P(SECTION, None, SHARD)
    in_specs = (rows, rows, P(), P()) + (layers,) * 7 + (pairs,) * 2
    out_specs = (both, both) + (columns,) * 7 + (P(SECTION, SHARD),) * 2
    return jax.shard_map(body, mesh=mesh, in_specs=in_specs, out_specs=out_specs, check_vma=False)
```

```python
from functools import partial

import jax
import jax.numpy as jnp
from jax import lax
from jax.experimental import pallas as pl
from jax.experimental.pallas import tpu as pltpu
from jax.sharding import Mesh, PartitionSpec as P

D = 768
HEADS = 12
HEAD_DIM = 64
FF = 3072
SEQ = 512
MICRO = 4

norm_eps = 1e-12
masked_score = -1e30
f32 = jnp.float32
bf16 = jnp.bfloat16
MIB = 1024 * 1024
FT = 512
RB = 256
UNIT = D // 2

SECTION, Z, CORE, SHARD = "section", "z", "core", "shard"
DATA = (Z, CORE, SHARD)
SWAP = [(0, 1), (1, 0)]

HBM = pl.BlockSpec(memory_space=pltpu.HBM)
ANY = pl.BlockSpec(memory_space=pl.ANY)
VM = pl.BlockSpec(memory_space=pltpu.VMEM)
SM = pl.BlockSpec(memory_space=pltpu.SMEM)


def sds(shape, dtype):
    return jax.ShapeDtypeStruct(shape, dtype)


def dot(a, b, ca=1, cb=0):
    return lax.dot_general(a, b, (((ca,), (cb,)), ((), ())), preferred_element_type=f32)


def params(mib):
    return pltpu.CompilerParams(vmem_limit_bytes=mib * MIB)


def cost(flops, bytes_accessed):
    return pl.CostEstimate(flops=flops, bytes_accessed=bytes_accessed, transcendentals=0)


def dma_sems(count):
    return pltpu.SemaphoreType.DMA((count,))


class Box:
    def __init__(self, names=(), refs=()):
        for n, r in zip(names, refs):
            setattr(self, n, r)

    def __getattr__(self, name):
        return None


def names_of(*tables):
    return [n for t in tables for n in t]


def shapes_of(*tables):
    return [sds(*e) for t in tables for e in t.values()]


def scratch_of(*tables, without=()):
    merged = {n: e for t in reversed(tables) for n, e in t.items() if n not in without}
    return list(merged), [pltpu.VMEM(*e) for e in merged.values()]


class Copies:
    def __init__(self, sems):
        self.sems, self.pending = sems, []

    def put(self, src, dst):
        if dst is not None:
            c = pltpu.make_async_copy(src, dst, self.sems.at[len(self.pending)])
            c.start()
            self.pending.append(c)

    def wait(self):
        for c in self.pending:
            c.wait()


def load(sems, now=4, **pairs):
    loads, copies = Box(), []
    for i, (name, (src, dst)) in enumerate(pairs.items()):
        copies.append(pltpu.make_async_copy(src, dst, sems.at[i]))
        setattr(loads, name, copies[-1])

    def start(some):
        for c in some:
            c.start()

    start(copies[:now])
    loads.later = lambda: start(copies[now:])
    return loads


def arrived(*copies):
    for c in copies:
        if c is not None:
            c.wait()


def live_rows(length, rows, cols, start=0):
    return lax.broadcasted_iota(jnp.int32, (rows, cols), 0) + start < length


def column_sum(v):
    return jnp.sum(v, axis=0, keepdims=True)


def gelu_and_slope(h):
    phi = 0.5 + 0.5 * lax.erf(h * 0.7071067811865476)
    return h * phi, phi + h * (jnp.exp(-0.5 * (h * h)) * 0.3989422804014327)


def qkv_step(x, wqkv, ab, qkv_t, loads):
    for j, ready in enumerate((loads.wq, loads.wk, loads.wv)):
        arrived(ready)
        if j == 0 and loads.later is not None:
            loads.later()
        part = dot(x[...], wqkv[:, j * D : (j + 1) * D])
        if j == 0:
            part = part + ab[0:1, :].astype(f32)
        elif j == 2:
            part = part + ab[1:2, :].astype(f32)
        low = part.astype(bf16)
        if j == 0:
            low = low * jnp.bfloat16(0.125)
        qkv_t[j * D : (j + 1) * D, :] = low.T


def head_rows(part, h):
    return slice(part * D + h * HEAD_DIM, part * D + (h + 1) * HEAD_DIM)


def attention_step(length, qkv_t, scores, expo, inv, ctx_t):
    dead_keys = lax.broadcasted_iota(jnp.int32, (16, SEQ), 1) >= length
    first_row = lax.broadcasted_iota(jnp.int32, (16, SEQ), 0) == 0
    mask_row = jnp.where(dead_keys & first_row, masked_score, 0.0).astype(bf16)
    one_row = jnp.where(first_row, 1.0, 0.0).astype(bf16)

    def score(h):
        k = jnp.concatenate([qkv_t[head_rows(1, h), :], mask_row], axis=0)
        q = jnp.concatenate([qkv_t[head_rows(0, h), :], one_row], axis=0)
        scores[h % 2] = dot(k, q, 0, 0)

    def context(h):
        c = dot(qkv_t[head_rows(2, h), :], expo[h]) * inv[h : h + 1, :]
        ctx_t[head_rows(0, h), :] = c.astype(bf16)

    score(0)
    for h in range(HEADS):
        if h + 1 < HEADS:
            score(h + 1)
        if h > 0:
            context(h - 1)
        for b in range(SEQ // RB):
            cols = slice(b * RB, (b + 1) * RB)
            s = scores[h % 2, :, cols]
            e = jnp.exp(s - jnp.max(s, axis=0, keepdims=True))
            inv[h : h + 1, cols] = 1.0 / column_sum(e)
            expo[h, :, cols] = e.astype(bf16)
    context(HEADS - 1)


def norm_rows(summed):
    centred = summed - jnp.mean(summed, axis=-1, keepdims=True)
    rstd = lax.rsqrt(jnp.mean(centred * centred, axis=-1, keepdims=True) + norm_eps)
    return centred * rstd, rstd


def first_norm_step(x, ctx_t, wout, ab, ng, ns, xh1, r1, first, nlow):
    for b in range(SEQ // RB):
        rows = slice(b * RB, (b + 1) * RB)
        summed = x[rows, :].astype(f32) + dot(ctx_t[:, rows].T, wout[...]) + ab[2:3, :].astype(f32)
        xh, rstd = norm_rows(summed)
        xh1[rows, :] = xh
        r1[rows, :] = jnp.broadcast_to(rstd, (RB, 128))
        one = xh * ng[0:1, :].astype(f32) + ns[0:1, :].astype(f32)
        first[rows, :] = one
        nlow[rows, :] = one.astype(bf16)


def feed_forward_step(nlow, win, wback, ib, hidden, act, slope, acc):
    count = FF // FT

    def into(f):
        cols = slice(f * FT, (f + 1) * FT)
        hidden[f % 2] = dot(nlow[...], win[:, cols]) + ib[:, cols].astype(f32)

    into(0)
    for f in range(count):
        cols = slice(f * FT, (f + 1) * FT)
        if f + 1 < count:
            into(f + 1)
        a, g = gelu_and_slope(hidden[f % 2])
        act[:, cols] = a.astype(bf16)
        if slope is not None:
            slope[:, cols] = g.astype(bf16)
    acc[...] = dot(act[...], wback[...])


def second_norm_step(length, first, acc, bb, ng, ns, xh2, r2, out, leave):
    for b in range(SEQ // RB):
        rows = slice(b * RB, (b + 1) * RB)
        xh, rstd = norm_rows(first[rows, :] + acc[rows, :] + bb[...].astype(f32))
        xh2[rows, :] = xh
        r2[rows, :] = jnp.broadcast_to(rstd, (RB, 128))
        y = xh * ng[1:2, :].astype(f32) + ns[1:2, :].astype(f32)
        out[rows, :] = jnp.where(live_rows(length, RB, D, b * RB), y, 0.0).astype(bf16)
        leave(pl.ds(b * RB, RB))


def norm_back(d, xh, rstd, gain):
    gd = d * gain.astype(f32)
    m1 = jnp.mean(gd, axis=-1, keepdims=True)
    m2 = jnp.mean(gd * xh, axis=-1, keepdims=True)
    return (gd - m1 - xh * m2) * rstd


def second_norm_back_step(length, d_rows, scale, xh2, r2, ng, acc, dmixed, small):
    small[...] = jnp.zeros((16, D), f32)
    for b in range(SEQ // RB):
        rows = slice(b * RB, (b + 1) * RB)
        dy = jnp.where(live_rows(length, RB, D, b * RB), d_rows[rows, :].astype(f32) * scale, 0.0)
        xh = xh2[rows, :]
        small[1:2, :] += column_sum(dy * xh)
        small[3:4, :] += column_sum(dy)
        d2 = norm_back(dy, xh, r2[rows, 0:1], ng[1:2, :])
        acc[rows, :] = d2
        low = d2.astype(bf16)
        dmixed[rows, :] = low
        small[4:5, :] += column_sum(low.astype(f32))


def feed_back_step(dmixed, wback, win, slope, dh, acc, small, arrive, leave):
    for f in range(FF // FT):
        cols = slice(f * FT, (f + 1) * FT)
        arrive(f)
        low = (dot(dmixed[...], wback[cols, :], 1, 1) * slope[:, cols].astype(f32)).astype(bf16)
        dh[:, cols] = low
        sums = column_sum(low.astype(f32))
        for piece in range(0, FT, RB):
            at = f * FT + piece
            small[8 + at // D : 9 + at // D, at % D : at % D + RB] = sums[:, piece : piece + RB]
    leave()
    acc[...] += dot(dh[...], win[...], 1, 1)


def first_norm_back_step(acc, xh1, r1, ng, dsum, dbranch, small):
    for b in range(SEQ // RB):
        rows = slice(b * RB, (b + 1) * RB)
        df = acc[rows, :]
        xh = xh1[rows, :]
        small[0:1, :] += column_sum(df * xh)
        small[2:3, :] += column_sum(df)
        d1 = norm_back(df, xh, r1[rows, 0:1], ng[0:1, :])
        dsum[rows, :] = d1
        low = d1.astype(bf16)
        dbranch[rows, :] = low
        small[5:6, :] += column_sum(low.astype(f32))


def context_back_step(wout, dbranch, dctx_t):
    dctx_t[...] = dot(wout[...], dbranch[...], 1, 1).astype(bf16)


def attention_back_step(heads, qkv_t, expo, inv, ctx_t, dctx_t, dprob, dqkv_t, arrive=lambda h: None):
    kept = {}

    def into(h):
        d_o = dctx_t[head_rows(0, h), :].astype(f32) * inv[h : h + 1, :]
        delta = column_sum(d_o * ctx_t[head_rows(0, h), :].astype(f32))
        low = d_o.astype(bf16)
        dprob[h % 2] = dot(qkv_t[head_rows(2, h), :], low, 0, 0)
        kept[h] = (low, delta)

    def out_of(h):
        low, delta = kept.pop(h)
        arrive(h)
        p = expo[h]
        ds = (p.astype(f32) * (dprob[h % 2] - delta)).astype(bf16)
        d_q = (dot(qkv_t[head_rows(1, h), :], ds) * 0.125).astype(bf16)
        d_k = dot(qkv_t[head_rows(0, h), :], ds, 1, 1).astype(bf16)
        dqkv_t[head_rows(0, h), :] = d_q
        dqkv_t[head_rows(1, h), :] = d_k
        dqkv_t[head_rows(2, h), :] = dot(low, p, 1, 1).astype(bf16)

    heads = list(heads)
    into(heads[0])
    for i, h in enumerate(heads):
        if i + 1 < len(heads):
            into(heads[i + 1])
        out_of(h)


def qkv_back_step(dqkv_t, dqkv, small):
    for j in range(3):
        low = dqkv_t[j * D : (j + 1) * D, :].T
        dqkv[:, j * D : (j + 1) * D] = low
        if j != 1:
            at = 6 + j // 2
            small[at : at + 1, :] = column_sum(low.astype(f32))


def input_back_step(dqkv, wqkv, dsum, din, leave=lambda rows: None):
    for b in range(SEQ // RB):
        rows = slice(b * RB, (b + 1) * RB)
        din[rows, :] = (dot(dqkv[rows, :], wqkv[...], 1, 1) + dsum[rows, :]).astype(bf16)
        leave(pl.ds(b * RB, RB))


ROWS16 = ((SEQ, D), bf16)
ROWS32 = ((SEQ, D), f32)
COLS16 = ((D, SEQ), bf16)
STD = ((SEQ, 128), f32)
WIDE16 = ((SEQ, FF), bf16)
QKV_T = ((3 * D, SEQ), bf16)
EXPO = ((HEADS, SEQ, SEQ), bf16)
INV = ((16, SEQ), f32)
SCORES = ((2, SEQ, SEQ), f32)
SMALL = ((16, D), f32)
HALF = ((SEQ, D // 2), bf16)
HALF_T = ((D // 2, SEQ), bf16)

OUT = dict(out=ROWS16)
SHARED = dict(
    x_own=HALF, x_send=HALF, ctx_own=HALF_T, ctx_send=HALF_T, nlow=ROWS16, act_own=((SEQ, FF // 2), bf16),
    act_send=((SEQ, FF // 2), bf16),
)
STORED = dict(
    qkv_t=QKV_T, expo=EXPO, inv=INV, ctx_t=COLS16, xh1=ROWS32, r1=STD, slope=WIDE16, xh2=ROWS32, r2=STD
)
NORM_OUTS = dict(dmixed=ROWS16)
BLOCK2 = ((2, SEQ, UNIT), bf16)
FFN_OUTS = dict(
    dh0=HALF, dh1=HALF, dh2=HALF, dh3=HALF, ds0=HALF, ds1=HALF, ds2=HALF, ds3=HALF, dbranch=ROWS16
)
ATT_OUTS = dict(
    dqkv0=BLOCK2, dqkv1=BLOCK2, dqkv2=BLOCK2, small=SMALL
)
DIN = dict(din=ROWS16)
NORM_MORE = dict(acc=ROWS32, small=SMALL)
FFN_MORE = dict(dctx_t=COLS16, dsum=ROWS32, small=SMALL)

WEIGHTS = dict(wqkv=((D, 3 * D), bf16), wout=((D, D), bf16), win=((D, FF), bf16), wback=((FF, D), bf16))
FORWARD = dict(
    x=ROWS16, qkv_t=QKV_T, scores=SCORES, expo=EXPO, inv=INV, ctx_t=COLS16, nlow=ROWS16, xh1=ROWS32, r1=STD,
    first=ROWS32, act=WIDE16, slope=WIDE16, xh2=ROWS32, r2=STD, out=ROWS16, acc=ROWS32,
)
BACK_FFN = dict(
    acc=ROWS32, dmixed=ROWS16, dh=WIDE16, dsum=ROWS32, dbranch=ROWS16, dctx_t=COLS16, small=SMALL
)
BACK_ATT = dict(dqkv_t=QKV_T, dqkv=((SEQ, 3 * D), bf16), din=ROWS16)


def halves(core, width):
    return (
        pl.ds(pl.multiple_of(core * width, 128), width),
        pl.ds(pl.multiple_of((1 - core) * width, 128), width),
    )


def weight_loads(v, wqkv, wout, win, wback):
    parts = [pl.ds(j * D, D) for j in range(3)]
    wq, wk, wv = [(wqkv.at[:, p], v.wqkv.at[:, p]) for p in parts]
    return dict(wq=wq, wk=wk, wv=wv, wout=(wout, v.wout), win=(win, v.win), wback=(wback, v.wback))


def forward_steps(v, w, o, length, core, copies, loads):
    own_d, other_d = halves(core, D // 2)
    own_f, other_f = halves(core, FF // 2)
    arrived(loads.x)
    copies.put(v.x.at[:, own_d], o.x_own)
    copies.put(v.x.at[:, other_d], o.x_send)
    qkv_step(v.x, v.wqkv, w.ab, v.qkv_t, loads)
    copies.put(v.qkv_t, o.qkv_t)
    attention_step(length, v.qkv_t, v.scores, v.expo, v.inv, v.ctx_t)
    copies.put(v.ctx_t.at[own_d, :], o.ctx_own)
    copies.put(v.ctx_t.at[other_d, :], o.ctx_send)
    copies.put(v.expo, o.expo)
    copies.put(v.inv, o.inv)
    copies.put(v.ctx_t, o.ctx_t)
    arrived(loads.wout)
    first_norm_step(v.x, v.ctx_t, v.wout, w.ab, w.ng, w.ns, v.xh1, v.r1, v.first, v.nlow)
    copies.put(v.nlow, o.nlow)
    copies.put(v.xh1, o.xh1)
    copies.put(v.r1, o.r1)
    arrived(loads.win, loads.wback)
    feed_forward_step(v.nlow, v.win, v.wback, w.ib, v.scores, v.act, v.slope, v.acc)
    copies.put(v.act.at[:, own_f], o.act_own)
    copies.put(v.act.at[:, other_f], o.act_send)
    copies.put(v.slope, o.slope)

    def leave(rows):
        if o.out is not None:
            copies.put(v.out.at[rows, :], o.out.at[rows, :])

    second_norm_step(length, v.first, v.acc, w.bb, w.ng, w.ns, v.xh2, v.r2, v.out, leave)
    copies.put(v.xh2, o.xh2)
    copies.put(v.r2, o.r2)


def leave_hidden(dh, o, core, copies):
    for refs, c in (((o.ds0, o.ds1, o.ds2, o.ds3), 1 - core), ((o.dh0, o.dh1, o.dh2, o.dh3), core)):
        for i, ref in enumerate(refs):
            half, block = i // 2, i % 2
            at = pl.multiple_of(half * (FF // 2) + c * (FF // 4) + block * UNIT, 128)
            copies.put(dh.at[:, pl.ds(at, UNIT)], ref)


def ffn_back_steps(v, w, o, core, copies):
    def leave():
        leave_hidden(v.dh, o, core, copies)

    feed_back_step(v.dmixed, v.wback, v.win, v.slope, v.dh, v.acc, v.small, lambda f: None, leave)
    first_norm_back_step(v.acc, v.xh1, v.r1, w.ng, v.dsum, v.dbranch, v.small)
    copies.put(v.dbranch, o.dbranch)
    context_back_step(v.wout, v.dbranch, v.dctx_t)


def leave_dqkv(v, o, copies):
    for u, ref in enumerate((o.dqkv0, o.dqkv1, o.dqkv2)):
        for half in range(2):
            copies.put(v.dqkv.at[:, pl.ds((3 * half + u) * UNIT, UNIT)], ref.at[half])
    copies.put(v.small, o.small)


def attention_back_end(v, o, copies):
    qkv_back_step(v.dqkv_t, v.dqkv, v.small)
    leave_dqkv(v, o, copies)
    input_back_step(
        v.dqkv, v.wqkv, v.dsum, v.din, lambda rows: copies.put(v.din.at[rows, :], o.din.at[rows, :])
    )


SMALL_WEIGHTS = dict(ab=0, ng=0, ns=0, ib=0, bb=0)


def here(lengths):
    z, core, shard = lax.axis_index(Z), lax.axis_index(CORE), lax.axis_index(SHARD)
    read = (z * 2 + core) * lax.axis_size(SHARD) + shard
    return jnp.where(lax.axis_index(SECTION) == 0, 1, 0), lengths[read], core


def first_kernel(names, out_names, lengths, x, wqkv, wout, win, wback, ab, ng, ns, ib, bb, *rest):
    n = len(out_names)
    o = Box(out_names, rest[:n])
    v = Box(names, rest[n:-2])
    w = Box(SMALL_WEIGHTS, (ab, ng, ns, ib, bb))
    live, length, core = here(lengths)

    @pl.when(live == 1)
    def _():
        loads = load(rest[-2], x=(x, v.x), **weight_loads(v, wqkv, wout, win, wback))
        copies = Copies(rest[-1])
        forward_steps(v, w, o, length, core, copies, loads)
        copies.wait()


def first_forward(lengths, x, weights, tables, name):
    without = () if STORED in tables else ("slope",)
    names, scratch = scratch_of(WEIGHTS, FORWARD, without=without)
    outs = shapes_of(*tables)
    return pl.pallas_call(
        partial(first_kernel, names, names_of(*tables)),
        out_shape=outs,
        in_specs=[SM, ANY] + [HBM] * 4 + [VM] * 5,
        out_specs=[HBM] * len(outs),
        scratch_shapes=scratch + [dma_sems(7), dma_sems(len(outs) + 1)],
        compiler_params=params(54),
        cost_estimate=cost(8 * 10**9, 36 * 10**6),
        name=name,
    )(lengths, x, *weights)


SECOND_OUTS = (OUT, SHARED, NORM_OUTS, FFN_OUTS, ATT_OUTS, DIN)


def second_kernel(names, scal, scale, x, cot, wqkv, wout, win, wback, ab, ng, ns, ib, bb, *rest):
    rest = rest[1 + len(SHARED) :]
    out_names = names_of(*SECOND_OUTS)
    n = len(out_names)
    o = Box(out_names, rest[:n])
    v = Box(names, rest[n:-2])
    w = Box(SMALL_WEIGHTS, (ab, ng, ns, ib, bb))

    @pl.when(scal[0] == 1)
    def _():
        length, core = scal[1], scal[2]
        loads = load(rest[-2], x=(x, v.x), **weight_loads(v, wqkv, wout, win, wback), cot=(cot, v.cot))
        copies = Copies(rest[-1])
        v.dsum, v.dh, v.dqkv_t = v.first, v.slope, v.qkv_t
        forward_steps(v, w, o, length, core, copies, loads)
        arrived(loads.cot)
        second_norm_back_step(length, v.cot, scale[0], v.xh2, v.r2, w.ng, v.acc, v.dmixed, v.small)
        copies.put(v.dmixed, o.dmixed)
        ffn_back_steps(v, w, o, core, copies)
        attention_back_step(range(HEADS), v.qkv_t, v.expo, v.inv, v.ctx_t, v.dctx_t, v.scores, v.dqkv_t)
        attention_back_end(v, o, copies)
        copies.wait()


def second_layer(scal, scale, x, cot, weights, shared):
    names, scratch = scratch_of(
        WEIGHTS, FORWARD, BACK_FFN, BACK_ATT, dict(cot=ROWS16), without=("dsum", "dh", "dqkv_t")
    )
    outs = shapes_of(*SECOND_OUTS)
    n_in = 13
    flat = pl.pallas_call(
        partial(second_kernel, names),
        out_shape=outs,
        in_specs=[SM, SM, ANY, ANY] + [HBM] * 4 + [VM] * 5 + [HBM] * len(shared),
        out_specs=[HBM] * len(outs),
        input_output_aliases={n_in + i: i for i in range(len(shared))},
        scratch_shapes=scratch + [dma_sems(8), dma_sems(len(outs) + 7)],
        compiler_params=params(57),
        cost_estimate=cost(20 * 10**9, 36 * 10**6),
        name="second_layer",
    )(scal, scale, x, cot, *weights, *shared)
    return Box(names_of(*SECOND_OUTS), flat)


def pick(source, table):
    return [getattr(source, n) for n in table]


def in_hbm(arrays):
    return [pltpu.with_memory_space_constraint(a, pltpu.HBM) for a in arrays]


def take_late(pairs, sems):
    copies = Copies(sems)
    for src, dst in pairs:
        copies.put(src, dst)
    copies.wait()


def norm_back_kernel(scal, d_rows, xh2, r2, ng, late, dmixed, acc, small, sems):
    @pl.when(scal[0] == 1)
    def _():
        second_norm_back_step(scal[1], d_rows, 1.0, xh2, r2, ng, acc, dmixed, small)

    @pl.when(scal[0] == 0)
    def _():
        take_late([(late, dmixed)], sems)


def first_norm_back(scal, d_rows, given, late):
    outs = shapes_of(NORM_OUTS, NORM_MORE)
    flat = pl.pallas_call(
        norm_back_kernel,
        out_shape=outs,
        in_specs=[SM, VM, VM, VM, VM, HBM],
        out_specs=[VM] * len(outs),
        scratch_shapes=[dma_sems(1)],
        compiler_params=params(8),
        cost_estimate=cost(2 * 10**10, 6 * 10**6),
        name="first_norm_back",
    )(scal, d_rows, given.xh2, given.r2, given.ng, *in_hbm([late.dmixed]))
    return flat[0], Box(NORM_MORE, flat[1:])


FFN_LOADS = dict(dmixed=0, wback=0, slope=0, win=0, acc=0, small=0, xh1=0, r1=0, wout=0, ng=0)


def ffn_back_kernel(scal, *rest):
    given = Box(FFN_LOADS, rest)
    rest = rest[len(FFN_LOADS) :]
    late = rest[: len(FFN_OUTS)]
    rest = rest[len(FFN_OUTS) :]
    o = Box(names_of(FFN_OUTS, FFN_MORE), rest)
    dh, acc, sems = rest[-3:]

    @pl.when(scal[0] == 1)
    def _():
        core = scal[2]
        copies = Copies(sems)
        acc[...] = given.acc[...]
        o.small[...] = given.small[...]

        def leave():
            leave_hidden(dh, o, core, copies)

        feed_back_step(given.dmixed, given.wback, given.win, given.slope, dh, acc, o.small, lambda f: None, leave)
        first_norm_back_step(acc, given.xh1, given.r1, given.ng, o.dsum, o.dbranch, o.small)
        context_back_step(given.wout, o.dbranch, o.dctx_t)
        copies.wait()

    @pl.when(scal[0] == 0)
    def _():
        take_late(zip(late, pick(o, FFN_OUTS)), sems)


def first_ffn_back(scal, given, late):
    outs = shapes_of(FFN_OUTS, FFN_MORE)
    flat = pl.pallas_call(
        ffn_back_kernel,
        out_shape=outs,
        in_specs=[SM] + [VM] * len(FFN_LOADS) + [HBM] * len(FFN_OUTS),
        out_specs=[VM] * len(outs),
        scratch_shapes=[pltpu.VMEM(*WIDE16), pltpu.VMEM(*ROWS32), dma_sems(len(FFN_OUTS))],
        compiler_params=params(14),
        cost_estimate=cost(6 * 10**9, 25 * 10**6),
        name="first_ffn_back",
    )(scal, *pick(given, FFN_LOADS), *in_hbm(pick(late, FFN_OUTS)))
    n = len(FFN_OUTS)
    return Box(FFN_OUTS, flat), Box(FFN_MORE, flat[n:])


ATT_FIRST = dict(qkv_t=0, expo=0, inv=0, ctx_t=0, dctx_t=0)
ATT_LATER = dict(small=0)


def att_back_kernel(names, scal, *rest):
    given = Box(names_of(ATT_FIRST, ATT_LATER), rest)
    rest = rest[len(ATT_FIRST) + len(ATT_LATER) :]
    late, rest = rest[: len(ATT_OUTS)], rest[len(ATT_OUTS) :]
    o = Box(ATT_OUTS, rest)
    v = Box(names, rest[len(ATT_OUTS) : -1])

    @pl.when(scal[0] == 1)
    def _():
        g = given
        attention_back_step(range(HEADS), g.qkv_t, g.expo, g.inv, g.ctx_t, g.dctx_t, v.scores, v.dqkv_t)
        v.small[...] = g.small[...]
        copies = Copies(rest[-1])
        qkv_back_step(v.dqkv_t, v.dqkv, v.small)
        leave_dqkv(v, o, copies)
        copies.wait()

    @pl.when(scal[0] == 0)
    def _():
        stages = [v.dqkv.at[:, pl.ds(i * UNIT, UNIT)] for i in range(6)] + [v.small]
        before = [late[u].at[half] for u in range(3) for half in range(2)] + list(late[3:])
        there = [r.at[half] for r in (o.dqkv0, o.dqkv1, o.dqkv2) for half in range(2)] + [o.small]
        take_late(zip(before, stages), rest[-1])
        take_late(zip(stages, there), rest[-1])


def first_att_back(scal, given, late):
    names, scratch = scratch_of(BACK_ATT, dict(scores=SCORES, small=SMALL), without=("din",))
    outs = [pltpu.HBM(*e) for e in ATT_OUTS.values()]
    flat = pl.pallas_call(
        partial(att_back_kernel, names),
        out_shape=outs,
        in_specs=[SM] + [VM] * (len(ATT_FIRST) + len(ATT_LATER)) + [HBM] * len(ATT_OUTS),
        out_specs=[HBM] * len(outs),
        scratch_shapes=scratch + [dma_sems(len(outs) + 3)],
        compiler_params=params(18),
        cost_estimate=cost(0, 0),
        name="first_att_back",
    )(scal, *pick(given, ATT_FIRST), *pick(given, ATT_LATER), *in_hbm(pick(late, ATT_OUTS)))
    return Box(ATT_OUTS, flat)


def input_back_kernel(scal, d0, d1, d2, wqkv, dsum, late, din, dqkv, w, ds, stage, sems):
    @pl.when(scal[0] == 1)
    def _():
        copies = Copies(sems)
        for u, ref in enumerate((d0, d1, d2)):
            for half in range(2):
                copies.put(ref.at[half], dqkv.at[:, pl.ds((3 * half + u) * UNIT, UNIT)])
        copies.put(wqkv, w)
        copies.put(dsum, ds)
        copies.wait()
        input_back_step(dqkv, w, ds, stage)

    @pl.when(scal[0] == 0)
    def _():
        take_late([(late, stage)], sems)

    take_late([(stage, din)], sems)


def first_input_back(scal, dqkv, wqkv, dsum, late):
    return pl.pallas_call(
        input_back_kernel,
        out_shape=pltpu.HBM(*ROWS16),
        in_specs=[SM] + [HBM] * 6,
        out_specs=HBM,
        scratch_shapes=[
            pltpu.VMEM((SEQ, 3 * D), bf16), pltpu.VMEM(*WEIGHTS["wqkv"]), pltpu.VMEM(*ROWS32), pltpu.VMEM(*ROWS16),
            dma_sems(8),
        ],
        compiler_params=params(16),
        cost_estimate=cost(0, 0),
        name="first_input_back",
    )(scal, *in_hbm(dqkv), *in_hbm([wqkv, dsum, late]))


def half_of_small(small, h):
    rows = [small[0:8, h * UNIT : (h + 1) * UNIT]]
    for j in range(4):
        at = h * (FF // 2) + j * UNIT
        rows.append(small[8 + at // D : 9 + at // D, at % D : at % D + UNIT])
    rows.append(jnp.zeros((4, UNIT), f32))
    return jnp.concatenate(rows, axis=0)


def grad_kernel(pieces, n_in, scal, *refs):
    ins, outs = refs[:n_in], refs[n_in:]
    keep_at = scal[3]
    for out, half in zip(outs, (1 - keep_at, keep_at)):
        at = 0
        for a1, a2, a_dim, a_start, a_size, b1, b2, b_start in pieces:
            block = slice(a_start, a_start + a_size)

            def left(i):
                return ins[i][:, block] if a_dim == 0 else ins[i][block, :]

            def right(i):
                if isinstance(i, tuple):
                    return jnp.where(half == 0, ins[i[0]][...], ins[i[1]][...])
                width = ins[i].shape[1] // 2
                return ins[i][:, pl.ds(pl.multiple_of(half * width + b_start, 128), UNIT)]

            total = dot(left(a1), right(b1), a_dim, 0) + dot(left(a2), right(b2), a_dim, 0)
            out[at : at + a_size, :] = total.astype(bf16)
            at += a_size


def grad_chunk(scal, operands, pieces, name):
    rows = sum(p[4] for p in pieces)
    return pl.pallas_call(
        partial(grad_kernel, pieces, len(operands)),
        out_shape=[sds((rows, UNIT), bf16)] * 2,
        in_specs=[SM] + [VM] * len(operands),
        out_specs=[VM] * 2,
        compiler_params=params(10),
        cost_estimate=cost(2 * 10**10, 6 * 10**6),
        name=name,
    )(scal, *operands)


def last_grads_kernel(scal, *refs):
    blocks, others = refs[7:13], refs[:7]
    sides = refs[13:17]
    stages, b, sems = refs[17:24], refs[24], refs[25]
    x1, x2, c1, c2, db1, db2, small = stages
    first, units, rest = Copies(sems.at[pl.ds(0, 2)]), Copies(sems.at[pl.ds(2, 6)]), Copies(sems.at[pl.ds(8, 5)])
    for i in range(2):
        first.put(others[i], stages[i])
    for u in range(3):
        for i in range(2):
            units.put(blocks[3 * i + u], b.at[u, i])
    for i in range(2, 7):
        rest.put(others[i], stages[i])
    keep_at = scal[3]
    sides = tuple(zip((1 - keep_at, keep_at), sides[0:2], sides[2:4]))
    first.wait()
    for u in range(3):
        arrived(*units.pending[2 * u : 2 * u + 2])
        for half, *outs in sides:
            total = dot(x1[...], b[u, 0, half], 0, 0) + dot(x2[...], b[u, 1, half], 0, 0)
            outs[u // 2][u % 2 * UNIT : (u % 2 + 1) * UNIT, :] = total.astype(bf16)
    rest.wait()
    for half, _, out in sides:
        cols = pl.ds(pl.multiple_of(half * UNIT, 128), UNIT)
        out[UNIT : 2 * UNIT, :] = (dot(c1[...], db1[:, cols]) + dot(c2[...], db2[:, cols])).astype(bf16)
        out[2 * UNIT : 2 * UNIT + 16, :] = jnp.where(half == 0, half_of_small(small[...], 0), half_of_small(small[...], 1)).astype(bf16)


def last_grads(scal, others, blocks):
    stages = (HALF, HALF, HALF_T, HALF_T, ROWS16, ROWS16, SMALL)
    return pl.pallas_call(
        last_grads_kernel,
        out_shape=[sds((2 * UNIT, UNIT), bf16)] * 2 + [sds((2 * UNIT + 16, UNIT), bf16)] * 2,
        in_specs=[SM] + [ANY] * 13,
        out_specs=[VM] * 4,
        scratch_shapes=[pltpu.VMEM(*e) for e in stages]
        + [pltpu.VMEM((3, 2, 2, SEQ, UNIT), bf16), dma_sems(13)],
        compiler_params=params(18),
        cost_estimate=cost(0, 0),
        name="last_grads",
    )(scal, *others, *blocks)


def place_kernel(moves, n_prev, n_out, scal, own, other, *rest):
    outs = rest[n_prev : n_prev + n_out]
    stage, sem = rest[-2:]
    core = scal[2]
    copies = Copies(sem)
    for i, (ref, c) in enumerate(((own, core), (other, 1 - core))):
        stage[i] = ref[...].astype(f32)
        for out, src, size, rows, row_step, col, col_step in moves:
            row = pl.multiple_of(rows + c * row_step, 8)
            column = pl.multiple_of(col + c * col_step, 128)
            copies.put(stage.at[i, pl.ds(src, size), :], outs[out].at[pl.ds(row, size), pl.ds(column, UNIT)])
    if n_out < len(rest) - 2 - n_prev:
        bias, gain, shift, hidden, last = rest[n_prev + n_out : -2]
        at = own.shape[0] - 16
        small = own[at : at + 16, :].astype(f32) + other[at : at + 16, :].astype(f32)
        gain[...] = small[0:2, :]
        shift[...] = small[2:4, :]
        last[...] = small[4:5, :]
        bias[0:1, :] = small[6:7, :]
        bias[1:2, :] = small[7:8, :]
        bias[2:3, :] = small[5:6, :]
        for j in range(4):
            hidden[:, j * UNIT : (j + 1) * UNIT] = small[8 + j : 9 + j, :]
    copies.wait()


SMALL_OUTS = ((3, UNIT), (2, UNIT), (2, UNIT), (1, FF // 2), (1, UNIT))


def place(scal, own, other, moves, shapes, previous, with_small=False):
    kept = [i for i, p in enumerate(previous) if p is not None]
    small = [sds(s, f32) for s in SMALL_OUTS] if with_small else []
    return pl.pallas_call(
        partial(place_kernel, moves, len(kept), len(shapes)),
        out_shape=[sds(s, f32) for s in shapes] + small,
        in_specs=[SM, VM, VM] + [HBM] * len(kept),
        out_specs=[HBM] * len(shapes) + [VM] * len(small),
        input_output_aliases={3 + j: i for j, i in enumerate(kept)},
        scratch_shapes=[pltpu.VMEM((2,) + own.shape, f32), dma_sems(2 * len(moves))],
        compiler_params=params(8),
        cost_estimate=cost(0, own.size * 12),
        name="place",
    )(scal, own, other, *[previous[i] for i in kept])


def add_kernel(start, a, b, out):
    rows = slice(start, start + out.shape[0])
    out[...] = (a[rows, :].astype(f32) + b[rows, :].astype(f32)).astype(bf16)


def added(a, b, start=0, size=None):
    rows = slice(start, start + (a.shape[0] if size is None else size))
    return (a[rows].astype(f32) + b[rows].astype(f32)).astype(bf16)


def take_kernel(takes, a, b, out):
    @pl.when(takes[0] == 1)
    def _():
        out[...] = a[...]

    @pl.when(takes[0] == 0)
    def _():
        out[...] = b[...]


def taken(takes, a, b):
    return jnp.where(takes[0] == 1, a, b)


def read_weights(lengths, assignment):
    member = assignment == jnp.arange(MICRO, dtype=jnp.int32)[None, :]
    counts = jnp.sum(jnp.where(member, lengths[:, None], 0), axis=0)
    token_total = jnp.sum(lengths).astype(f32)
    scales = token_total / (MICRO * counts.astype(f32))
    return jnp.sum(jnp.where(member, scales[None, :], 0.0), axis=1)


class Order:
    def __init__(self):
        self.last = None

    def after(self, value):
        if self.last is not None:
            value, self.last = lax.optimization_barrier((value, self.last))
        return value

    def done(self, value):
        self.last = value
        return value


class Sums:
    def __init__(self, scal, order, z_index, z_count, shapes):
        self.scal, self.order, self.z_index, self.z_count, self.shapes = scal, order, z_index, z_count, shapes
        self.value, self.moving, self.keep, self.results, self.small = {}, {}, {}, {}, None
        half = z_count // 2
        self.stages = [[self.shard_done, partial(self.inward, hop=0)]]
        for hop in range(half - 1):
            self.stages.append([self.add, self.middle if hop + 2 == half else partial(self.inward, hop=hop + 1)])
        self.stages.append([self.add, partial(self.outward, hop=half - 2)])
        for hop in range(half - 2, -1, -1):
            after = partial(self.outward, hop=hop - 1) if hop > 0 else self.core
            self.stages.append([partial(self.take, hop=hop), after])
        self.stages.append([self.place])

    def start(self, pair, sizes):
        moving, at = lax.ppermute(pair[0], SHARD, SWAP), 0
        for size in sizes:
            i = len(self.keep)
            self.keep[i], self.moving[i] = pair[1], (moving, at, size)
            at += size

    def tick(self, t):
        for stage in (4, 3) if t == len(PLACES) + 2 else range(5):
            for i in range(len(PLACES)):
                if t == i + stage - (stage == 0 and i > 3):
                    for step in self.stages[stage]:
                        step(i)

    def shard_done(self, i):
        moving, at, size = self.moving[i]
        self.value[i] = self.order.done(added(self.order.after(moving), self.keep[i], at, size))

    def inward(self, i, hop):
        last = self.z_count - 1
        self.moving[i] = lax.ppermute(self.value[i], Z, [(hop, hop + 1), (last - hop, last - 1 - hop)])

    def add(self, i):
        self.value[i] = self.order.done(added(self.value[i], self.order.after(self.moving[i])))

    def middle(self, i):
        half = self.z_count // 2
        self.moving[i] = lax.ppermute(self.value[i], Z, [(half - 1, half), (half, half - 1)])

    def outward(self, i, hop):
        last = self.z_count - 1
        self.moving[i] = lax.ppermute(self.value[i], Z, [(hop + 1, hop), (last - 1 - hop, last - hop)])

    def take(self, i, hop):
        takes = ((self.z_index == hop) | (self.z_index == self.z_count - 1 - hop)).astype(jnp.int32)[None]
        self.value[i] = self.order.done(taken(takes, self.order.after(self.moving[i]), self.value[i]))

    def core(self, i):
        self.moving[i] = lax.ppermute(self.value[i], CORE, SWAP)

    def place(self, i):
        targets, moves, with_small = PLACES[i]
        flat = place(
            self.scal, self.value[i], self.order.after(self.moving[i]), moves, [self.shapes[t] for t in targets],
            [self.results.get(t) for t in targets], with_small,
        )
        self.order.done(flat[0])
        for t, r in zip(targets, flat):
            self.results[t] = r
        if with_small:
            self.small = flat[len(targets) :]


G_BACK, G_IN, G_QKV, G_OUT = range(4)
PLACES = (
    ((G_BACK,), ((0, 0, D, 0, FF // 2, 0, 0),), False),
    ((G_BACK,), ((0, 0, D, D, FF // 2, 0, 0),), False),
    ((G_IN,), ((0, 0, D, 0, 0, 0, FF // 4),), False),
    ((G_IN,), ((0, 0, D, 0, 0, UNIT, FF // 4),), False),
    ((G_QKV,), ((0, 0, UNIT, 0, UNIT, 0, 0), (0, UNIT, UNIT, 0, UNIT, UNIT, 0)), False),
    ((G_QKV, G_OUT), ((0, 0, UNIT, 0, UNIT, 2 * UNIT, 0), (1, UNIT, UNIT, 0, UNIT, 0, 0)), True),
)


def sums_by_collectives(pairs, small, shard, shard_count):
    side = [[p[1] for p in pairs], [p[0] for p in pairs]]
    back = jnp.concatenate([jnp.concatenate(s[0:2], axis=0) for s in side], axis=1)
    inner = jnp.stack([jnp.concatenate([s[2][:D], s[2][D:]], axis=1) for s in side], axis=1)
    qkv = jnp.concatenate([part for s in side for part in (s[3][:UNIT], s[3][UNIT:], s[4][:UNIT])], axis=1)
    out = jnp.concatenate([s[4][UNIT : 2 * UNIT] for s in side], axis=1)

    def mine(whole):
        width = whole.shape[1] // shard_count
        return lax.dynamic_slice_in_dim(whole, shard * width, width, 1)

    def by_rows(quarter):
        return mine(lax.all_gather(lax.psum(quarter.astype(f32), (Z, SHARD)), CORE, axis=0, tiled=True))

    inner = lax.all_gather(lax.psum(inner.astype(f32), (Z, SHARD)), CORE, axis=2).reshape(D, FF)
    total = lax.psum(small, DATA)
    part = mine(total)
    hidden = mine(total[8:12].reshape(1, FF))
    results = {G_BACK: by_rows(back), G_IN: mine(inner), G_QKV: by_rows(qkv), G_OUT: by_rows(out)}
    return results, (jnp.stack([part[6], part[7], part[5]]), part[0:2], part[2:4], hidden, part[4:5])


def body(
    block_input, cotangent, lengths, assignment, qkv_weight, out_weight, in_weight, back_weight, attn_bias, norm_gain,
    norm_shift, in_bias, back_bias,
):
    section = lax.axis_index(SECTION)
    z_index, core, shard = lax.axis_index(Z), lax.axis_index(CORE), lax.axis_index(SHARD)
    z_count, shard_count = lax.axis_size(Z), lax.axis_size(SHARD)
    weights = (
        qkv_weight[0], out_weight[0], in_weight[0], back_weight[0], attn_bias[0], norm_gain[0], norm_shift[0], in_bias,
        back_bias,
    )
    keep_at = shard if shard_count == 2 else 0
    (out,) = first_forward(lengths, block_input, weights, (OUT,), "first_forward")
    received = lax.ppermute(out, SECTION, [(0, 1)])
    lengths, assignment, _ = lax.optimization_barrier((lengths, assignment, out))
    data_index = (z_index * 2 + core) * shard_count + shard
    length = lax.dynamic_index_in_dim(lengths, data_index, 0, keepdims=False)
    own_scale = lax.dynamic_slice_in_dim(read_weights(lengths, assignment), data_index, 1)

    def scalars(live):
        return jnp.stack([live.astype(jnp.int32), length, core, jnp.asarray(keep_at, jnp.int32)])

    def core_swap(array):
        return lax.ppermute(array, CORE, SWAP)

    at_first, at_second = scalars(section == 0), scalars(section == 1)
    kept = first_forward(lengths, block_input, weights, (SHARED, STORED), "first_forward_kept")
    given = Box(names_of(SHARED, STORED), kept)
    late = second_layer(at_second, own_scale, *in_hbm([received]), cotangent, weights, [out, *kept[: len(SHARED)]])
    returned = lax.ppermute(late.din, SECTION, [(1, 0)])
    from_peer = [core_swap(a) for a in (late.act_send, late.nlow, late.x_send, late.ctx_send)]
    returned, from_peer = lax.optimization_barrier((returned, from_peer))
    act_peer, nlow_peer, x_peer, ctx_peer = from_peer

    order = Order()
    shapes = {
        G_QKV: (D, 3 * D // shard_count), G_OUT: (D, D // shard_count), G_IN: (D, FF // shard_count),
        G_BACK: (FF, D // shard_count),
    }
    sums = Sums(at_first, order, z_index, z_count, shapes)
    pairs = []

    def start(pair, sizes):
        pairs.append(pair)
        if shard_count == 2:
            sums.start(pair, sizes)

    def grad(operands, pieces, name):
        pair = grad_chunk(order.after(at_first), operands, pieces, name)
        order.done(pair[0])
        start(pair, (D,) * len(pieces))

    def tick(*args):
        if shard_count == 2:
            sums.tick(*args)

    given.ng, given.wqkv, given.wout, given.win, given.wback = norm_gain[0], *weights[:4]
    given.dmixed, more = first_norm_back(at_first, returned, given, late)
    given.acc, given.small = more.acc, more.small
    dmixed_peer = core_swap(given.dmixed)
    for k in range(2):
        grad((late.act_own, act_peer, given.dmixed, dmixed_peer), ((0, 1, 0, k * D, D, 2, 3, 0),), "grad_back")
    ffn, more = first_ffn_back(order.after(at_first), given, late)
    order.done(ffn.dbranch)
    given.dctx_t, given.dsum, given.small = more.dctx_t, more.dsum, more.small
    own = (ffn.dh0, ffn.dh1, ffn.dh2, ffn.dh3)
    peer = [core_swap(a) for a in (ffn.ds0, ffn.ds1, ffn.ds2, ffn.ds3)]
    tick(0)
    operands = (late.nlow, nlow_peer, *own, *peer)
    grad(operands, ((0, 1, 0, 0, D, (2, 4), (6, 8), 0), (0, 1, 0, 0, D, (3, 5), (7, 9), 0)), "grad_in")
    dbranch_peer = core_swap(ffn.dbranch)
    go, dbranch_peer = order.after((at_first, dbranch_peer))
    att = first_att_back(go, given, late)
    order.done(att.small)
    tick(1)
    own = (att.dqkv0, att.dqkv1, att.dqkv2)
    peer = [core_swap(a) for a in own]

    x_own, ctx_own, x_peer, ctx_peer, small = in_hbm([late.x_own, late.ctx_own, x_peer, ctx_peer, att.small])
    others = (x_own, x_peer, ctx_own, ctx_peer, ffn.dbranch, dbranch_peer, small)
    last = last_grads(order.after(at_first), others, (*in_hbm(own), *peer))
    order.done(last[0])
    start(last[0:2], (D,))
    start(last[2:4], (D + 16,))
    if shard_count == 2:
        for t in range(2, len(PLACES) + len(sums.stages) - 1):
            tick(t)
            if t == 7:
                din = order.done(first_input_back(order.after(at_first), own, weights[0], given.dsum, late.din))
        results, small = sums.results, sums.small
    else:
        din = first_input_back(at_first, own, weights[0], given.dsum, late.din)
        results, small = sums_by_collectives(pairs, att.small, shard, shard_count)
    return (
        late.out[None], din[None], results[G_QKV][None], results[G_OUT][None], results[G_IN][None],
        results[G_BACK][None], small[0][None], small[1][None], small[2][None], small[3], small[4],
    )


def solution(mesh):
    sections, groups, shards = mesh.devices.shape
    mesh = Mesh(mesh.devices.reshape(sections, groups // 2, 2, shards), (SECTION, Z, CORE, SHARD))
    rows, layers, pairs = P(DATA, None), P(SECTION, None, None), P(SECTION, None)
    both, columns = P(SECTION, DATA, None), P(SECTION, None, SHARD)
    in_specs = (rows, rows, P(), P()) + (layers,) * 7 + (pairs,) * 2
    out_specs = (both, both) + (columns,) * 7 + (P(SECTION, SHARD),) * 2
    return jax.shard_map(body, mesh=mesh, in_specs=in_specs, out_specs=out_specs, check_vma=False)
```
